32 devices in a mesh: section: 4 (over y, x), dp: 8 (over z, core).
Axes of the slice: x: 2, y: 2, z: 4, core: 2. Of those that a mesh axis runs over, the one named last changes fastest.
Arguments:
- nbr_embed: bfloat16 [8, 4, 128, 896], P('dp', None, 'section'), may hold values from -140 to 140
- enc_weight: bfloat16 [896, 896], replicated, may hold values from -0.1875 to 0.1875
- enc_gain: float32 [896], replicated, may hold values from 0.1 to 1.9
- kv_weight: bfloat16 [4, 4096, 896], P('section'), may hold values from -0.1875 to 0.1875
- queries: bfloat16 [4, 1024, 2048], P('section', 'dp'), may hold values from -6 to 6
- pos_bias: bfloat16 [4, 16, 64, 256], P('section'), may hold values from -8 to 240
- nbr_ids: int32 [8, 2, 2], P('dp'), may hold values from 0 to 3
- ctx_grad: bfloat16 [4, 1024, 2048], P('section', 'dp'), may hold values from -12 to 12
Outputs:
- q_grad: bfloat16 [4, 1024, 2048], P('section', 'dp')
- kv_weight_grad: float32 [4, 4096, 896], P('section', 'dp')
- enc_weight_grad: float32 [896, 896], P('section')
- enc_gain_grad: float32 [896], replicated
- embed_grad: bfloat16 [8, 4, 128, 896], P('dp', None, 'section')
The draws below stay inside these ranges and needn't reach their ends.
All inputs are finite; a program needn't handle non-finite values.
Results may differ from the reference program's by a relative error of at most 0.02.
Values may be sent and summed in bfloat16 or wider, within the bound.
No kernel may reach another device: no remote copies, remote signals or barrier semaphores. Data moves between devices by JAX's collectives and lax.ppermute only.
A program may use at most 128 MiB of HBM per device.

```python
import math
import jax
import jax.numpy as jnp
from jax import lax

HEADS = 16
HEAD = 128
ENC_D = 896
BLOCK = 64
NBR = 2
NLEN = 128
TOK_DEV = 128
NSET = 4
TOKENS = 1024
N_SECTION = 4
N_DP = 8


def draw_nbr_embed(key, part):
    full_shape = (N_DP, NSET, NLEN, ENC_D)
    keys_list = jax.random.split(key, 3)
    col_scale = jnp.exp(jax.random.uniform(keys_list[2], (1, 1, 1, ENC_D), jnp.float32, -0.5 * math.log(10.0), 0.5 * math.log(10.0)))
    row_scale = jnp.exp(jax.random.uniform(keys_list[1], (N_DP, NSET, NLEN, 1), jnp.float32, 0.0, math.log(10.0)))
    base_vals = jnp.clip(jax.random.normal(keys_list[0], full_shape, jnp.float32), -4.0, 4.0)
    return (base_vals * row_scale * col_scale).astype(jnp.bfloat16)


def draw_pos_bias(key, part):
    key_rows = NBR * NLEN
    full_shape = (N_SECTION, HEADS, BLOCK, key_rows)
    keys_list = jax.random.split(key, 1)
    result = jnp.clip(jax.random.normal(keys_list[0], full_shape, jnp.float32), -6.0, 6.0)
    return result.astype(jnp.bfloat16)


def plant(drawn, stream_key, low, top_value):
    longest = drawn.shape.index(max(drawn.shape))
    spots = []
    for shift in (0, 1):
        where = [jax.random.randint(jax.random.fold_in(stream_key, axis), (), 0, length) for axis, length in enumerate(drawn.shape)]
        where[longest] = (where[longest] + shift) % drawn.shape[longest]
        spots.append(tuple(where))
    return drawn.at[spots[0]].set(low).at[spots[1]].set(top_value)


def block_levels(own_key, extent, cuts, low, top_value):
    loudness = 1.0
    for axis_at, blocks in cuts:
        heights = jax.random.uniform(jax.random.fold_in(jax.random.fold_in(own_key, 6), axis_at), (blocks,), jnp.float32, low / len(cuts), top_value / len(cuts))
        loudness = loudness * jnp.repeat(jnp.exp(heights), extent[axis_at] // blocks).reshape((-1,) + (1,) * (len(extent) - 1 - axis_at))
    return loudness


def scatter_about(rng, extent, spread, reach, cuts=(), kind=jnp.bfloat16):
    values = jax.random.normal(rng, extent, jnp.float32) * spread
    if len(cuts) > 0:
        values = block_levels(rng, extent, cuts, -0.22, 0.18) * values
    return jnp.clip(values, min=-reach, max=reach).astype(kind)


def setup_inputs(seed: int = 0) -> dict:
    keys = jax.random.split(jax.random.key(seed), 9)
    return {
        "nbr_embed": draw_nbr_embed(jax.random.fold_in(keys[8], 71), 0),
        "enc_weight": scatter_about(keys[1], (ENC_D, ENC_D), ENC_D ** -0.5, 0.1875),
        "enc_gain": jnp.clip(1.0 + 0.18 * jax.random.normal(keys[2], (ENC_D,), jnp.float32), 0.1, 1.9),
        "kv_weight": scatter_about(keys[3], (N_SECTION, 2 * HEADS * HEAD, ENC_D), ENC_D ** -0.5, 0.1875, ((0, 4),)),
        "queries": scatter_about(keys[4], (N_SECTION, TOKENS, HEADS * HEAD), 1.0, 6.0, ((0, 4), (1, 8))),
        "pos_bias": draw_pos_bias(jax.random.fold_in(keys[8], 71), 0),
        "nbr_ids": plant(jax.random.randint(keys[6], (N_DP, TOK_DEV // BLOCK, NBR), 0, NSET), jax.random.fold_in(keys[6], 1), 0, NSET - 1).astype(jnp.int32),
        "ctx_grad": scatter_about(keys[7], (N_SECTION, TOKENS, HEADS * HEAD), 2.0, 12.0, ((0, 4), (1, 8))),
    }


eps_norm = 1e-06

def replica_layer(weights, query_blk, bias_blk, ids_blk, grad_blk, encoded_rows):
    head_width = HEADS * HEAD
    key_rows = NBR * NLEN
    blocks = TOK_DEV // BLOCK
    factor = 1.0 / math.sqrt(HEAD)
    projected = lax.dot_general(encoded_rows, weights, (((1,), (1,)), ((), ())), preferred_element_type=jnp.float32).astype(jnp.bfloat16)
    projected = projected.reshape(NSET, NLEN, 2 * head_width)
    selector = (ids_blk[:, :, None] == jnp.arange(NSET, dtype=jnp.int32)[None, None, :]).astype(jnp.float32)
    chosen = jnp.einsum('cne,eld->cnld', selector, projected.astype(jnp.float32)).astype(jnp.bfloat16)
    chosen = chosen.reshape(blocks, key_rows, 2 * head_width)
    keys_all = chosen[:, :, :head_width].reshape(blocks, key_rows, HEADS, HEAD).astype(jnp.float32)
    values_all = chosen[:, :, head_width:].reshape(blocks, key_rows, HEADS, HEAD).astype(jnp.float32)
    query_all = query_blk.reshape(blocks, BLOCK, HEADS, HEAD).astype(jnp.float32)
    upstream = grad_blk.reshape(blocks, BLOCK, HEADS, HEAD).astype(jnp.float32)
    scores = jnp.einsum('cqhd,ckhd->chqk', query_all, keys_all) * factor + bias_blk.astype(jnp.float32)[None]
    row_peak = lax.optimization_barrier(jnp.max(scores, axis=-1, keepdims=True))
    exp_scores = jnp.exp(scores - row_peak)
    attn_probs = exp_scores / lax.optimization_barrier(jnp.sum(exp_scores, axis=-1, keepdims=True))
    probs_low = attn_probs.astype(jnp.bfloat16)
    grad_probs = jnp.einsum('cqhd,ckhd->chqk', upstream, values_all)
    row_inner = lax.optimization_barrier(jnp.sum(attn_probs * grad_probs, axis=-1, keepdims=True))
    grad_scores = (attn_probs * (grad_probs - row_inner)).astype(jnp.bfloat16).astype(jnp.float32)
    grad_query = (jnp.einsum('chqk,ckhd->cqhd', grad_scores, keys_all) * factor).astype(jnp.bfloat16)
    grad_query = grad_query.reshape(TOK_DEV, head_width)
    grad_keys = jnp.einsum('chqk,cqhd->ckhd', grad_scores, query_all) * factor
    grad_values = jnp.einsum('chqk,cqhd->ckhd', probs_low.astype(jnp.float32), upstream)
    grad_chosen = jnp.concatenate([grad_keys.reshape(blocks, key_rows, head_width), grad_values.reshape(blocks, key_rows, head_width)], axis=-1)
    grad_chosen = grad_chosen.reshape(blocks, NBR, NLEN, 2 * head_width)
    grad_set = jnp.einsum('cne,cnld->eld', selector, grad_chosen).astype(jnp.bfloat16)
    grad_set = grad_set.reshape(NSET * NLEN, 2 * head_width)
    grad_weights = lax.dot_general(grad_set, encoded_rows, (((0,), (0,)), ((), ())), preferred_element_type=jnp.float32)
    grad_weights = lax.optimization_barrier(grad_weights.astype(jnp.bfloat16)).astype(jnp.float32)
    grad_encoded = jnp.dot(grad_set, weights, preferred_element_type=jnp.float32)
    return (grad_query, grad_weights, grad_encoded)

def reference(nbr_embed, enc_weight, enc_gain, kv_weight, queries, pos_bias, nbr_ids, ctx_grad):
    head_width = HEADS * HEAD
    flat_rows = nbr_embed.reshape(N_DP * NSET * NLEN, ENC_D)
    mixed_rows = flat_rows.astype(jnp.float32) + jnp.dot(flat_rows, enc_weight, preferred_element_type=jnp.float32)
    inverse = lax.rsqrt(lax.optimization_barrier(jnp.mean(mixed_rows * mixed_rows, axis=-1, keepdims=True)) + eps_norm)
    normed = mixed_rows * inverse
    encoded = (normed * enc_gain[None, :]).astype(jnp.bfloat16).reshape(N_DP, NSET * NLEN, ENC_D)
    query_rep = queries.reshape(N_SECTION, N_DP, TOK_DEV, head_width)
    grad_rep = ctx_grad.reshape(N_SECTION, N_DP, TOK_DEV, head_width)

    def section_step(grad_total, section_inputs):
        weights, query_section, bias_section, grad_section = section_inputs

        def replica_step(running, replica_inputs):
            query_blk, ids_blk, grad_blk, encoded_rows = replica_inputs
            grad_query, grad_weights, grad_encoded = replica_layer(weights, query_blk, bias_section, ids_blk, grad_blk, encoded_rows)
            return (running + grad_weights, (grad_query, grad_encoded))
        zero_weights = jnp.zeros((2 * head_width, ENC_D), jnp.float32)
        weight_sum, (query_grads, encoded_grads) = lax.scan(replica_step, zero_weights, (query_section, nbr_ids, grad_section, encoded))
        return (grad_total + encoded_grads, (query_grads, weight_sum))
    zero_grad = jnp.zeros((N_DP, NSET * NLEN, ENC_D), jnp.float32)
    grad_encoded, (query_grads, kv_grads) = lax.scan(section_step, zero_grad, (kv_weight, query_rep, pos_bias, grad_rep))
    q_grad = query_grads.reshape(N_SECTION, N_DP * TOK_DEV, head_width)
    grad_flat = grad_encoded.reshape(N_DP * NSET * NLEN, ENC_D)
    gain_grad = lax.optimization_barrier(jnp.sum(grad_flat * normed, axis=0))
    grad_normed = grad_flat * enc_gain[None, :]
    grad_mixed = inverse * (grad_normed - normed * lax.optimization_barrier(jnp.mean(grad_normed * normed, axis=-1, keepdims=True)))
    grad_low = grad_mixed.astype(jnp.bfloat16)
    embed_grad = grad_mixed + lax.dot_general(grad_low, enc_weight, (((1,), (1,)), ((), ())), preferred_element_type=jnp.float32)
    embed_grad = embed_grad.astype(jnp.bfloat16).reshape(N_DP, NSET, NLEN, ENC_D)
    weight_grad = lax.dot_general(flat_rows, grad_low, (((0,), (0,)), ((), ())), preferred_element_type=jnp.float32)
    return (q_grad, kv_grads, weight_grad, gain_grad, embed_grad)
```

```python
import functools
import math

import jax
import jax.numpy as jnp
from jax import lax
from jax.experimental import pallas as pl
from jax.experimental.pallas import tpu as pltpu
from jax.sharding import PartitionSpec as P

HEADS = 16
HEAD = 128
ENC_D = 896
BLOCK = 64
NBR = 2
NLEN = 128
TOK_DEV = 128
NSET = 4
PAIR = 2
EXTRA = 16

eps_norm = 1e-06
F32 = jnp.float32
BF16 = jnp.bfloat16


def mm(a, b):
    return lax.dot_general(a, b, (((1,), (0,)), ((), ())), preferred_element_type=F32)


def mm_nt(a, b):
    return lax.dot_general(a, b, (((1,), (1,)), ((), ())), preferred_element_type=F32)


def mm_tn(a, b):
    return lax.dot_general(a, b, (((0,), (0,)), ((), ())), preferred_element_type=F32)


def layer_kernel(
    n_sec, ids, rows_ref, encw_ref, gain_ref, w_ref, q_ref, bias_ref, up_ref,
    qg_ref, kvg_ref, ge_ref, enc, proj, total, gset, acc,
):
    step = pl.program_id(0)
    part = NLEN // n_sec
    blocks = TOK_DEV // BLOCK
    width = PAIR * HEAD
    factor = 1.0 / math.sqrt(HEAD)

    @pl.when(step == 0)
    def _():
        for s in range(n_sec):
            for e in range(NSET):
                enc[pl.ds(e * NLEN + s * part, part), :] = rows_ref[s, pl.ds(e * part, part), :]
        for e in range(NSET):
            span = pl.ds(e * NLEN, NLEN)
            raw = enc[span, :]
            mixed = raw.astype(F32) + mm(raw, encw_ref[...])
            inverse = lax.rsqrt(jnp.mean(mixed * mixed, axis=-1, keepdims=True) + eps_norm)
            enc[span, :] = ((mixed * inverse) * gain_ref[...]).astype(BF16)
        acc[...] = jnp.zeros_like(acc)

    encoded = enc[...]
    proj[0] = mm_nt(encoded, w_ref[0]).astype(BF16)
    proj[1] = mm_nt(encoded, w_ref[1]).astype(BF16)
    total[...] = jnp.zeros_like(total)
    for c in range(blocks):
        spans = [pl.ds(pl.multiple_of(ids[c, n] * NLEN, NLEN), NLEN) for n in range(NBR)]
        tok = slice(c * BLOCK, (c + 1) * BLOCK)
        for h in range(PAIR):
            col = slice(h * HEAD, (h + 1) * HEAD)
            keys = jnp.concatenate([proj[0, s, col] for s in spans], axis=0)
            values = jnp.concatenate([proj[1, s, col] for s in spans], axis=0)
            query = q_ref[tok, col]
            upstream = up_ref[tok, col]
            scores = mm_nt(query, keys) * factor + bias_ref[h].astype(F32)
            peak = jnp.max(scores, axis=-1, keepdims=True)
            exps = jnp.exp(scores - peak)
            probs = exps / jnp.sum(exps, axis=-1, keepdims=True)
            dprobs = mm_nt(upstream, values)
            inner = jnp.sum(probs * dprobs, axis=-1, keepdims=True)
            dscores = (probs * (dprobs - inner)).astype(BF16)
            qg_ref[tok, col] = (mm(dscores, keys) * factor).astype(BF16)
            dkeys = mm_tn(dscores, query) * factor
            dvalues = mm_tn(probs.astype(BF16), upstream)
            for n, s in enumerate(spans):
                total[0, s, col] += dkeys[n * NLEN:(n + 1) * NLEN]
                total[1, s, col] += dvalues[n * NLEN:(n + 1) * NLEN]
    gset[...] = total[...].astype(BF16)
    for k in range(2):
        kvg_ref[k] = mm_tn(gset[k], encoded).astype(BF16)
    acc[...] += mm(gset[0], w_ref[0]) + mm(gset[1], w_ref[1])

    @pl.when(step == pl.num_programs(0) - 1)
    def _():
        for s in range(n_sec):
            for e in range(NSET):
                ge_ref[s, pl.ds(e * part, part), :] = acc[pl.ds(e * NLEN + s * part, part), :].astype(BF16)


def layer(n_sec, ids, rows, enc_weight, gain, weights, queries, bias, upstream):
    head_width = HEADS * HEAD
    width = PAIR * HEAD
    all_rows = NSET * NLEN
    part = all_rows // n_sec
    fixed2 = lambda i, ids: (0, 0)
    fixed3 = lambda i, ids: (0, 0, 0)
    return pl.pallas_call(
        functools.partial(layer_kernel, n_sec),
        grid_spec=pltpu.PrefetchScalarGridSpec(
            num_scalar_prefetch=1,
            grid=(HEADS // PAIR,),
            in_specs=[
                pl.BlockSpec((n_sec, part, ENC_D), fixed3),
                pl.BlockSpec((ENC_D, ENC_D), fixed2),
                pl.BlockSpec((1, ENC_D), fixed2),
                pl.BlockSpec((2, width, ENC_D), lambda i, ids: (0, i, 0)),
                pl.BlockSpec((TOK_DEV, width), lambda i, ids: (0, i)),
                pl.BlockSpec((PAIR, BLOCK, NBR * NLEN), lambda i, ids: (i, 0, 0)),
                pl.BlockSpec((TOK_DEV, width), lambda i, ids: (0, i)),
            ],
            out_specs=[
                pl.BlockSpec((TOK_DEV, width), lambda i, ids: (0, i)),
                pl.BlockSpec((2, width, ENC_D), lambda i, ids: (0, i, 0)),
                pl.BlockSpec((n_sec, part, ENC_D), fixed3),
            ],
            scratch_shapes=[
                pltpu.VMEM((all_rows, ENC_D), BF16),
                pltpu.VMEM((2, all_rows, width), BF16),
                pltpu.VMEM((2, all_rows, width), F32),
                pltpu.VMEM((2, all_rows, width), BF16),
                pltpu.VMEM((all_rows, ENC_D), F32),
            ],
        ),
        out_shape=[
            jax.ShapeDtypeStruct((TOK_DEV, head_width), BF16),
            jax.ShapeDtypeStruct((2, head_width, ENC_D), BF16),
            jax.ShapeDtypeStruct((n_sec, part, ENC_D), BF16),
        ],
        compiler_params=pltpu.CompilerParams(
            vmem_limit_bytes=40 * 1024 * 1024, dimension_semantics=("arbitrary",)
        ),
    )(ids, rows, enc_weight, gain, weights.reshape(2, head_width, ENC_D), queries, bias, upstream)


def split_rows(row, count, rounded):
    high = rounded(row)
    low = row - high
    at = lax.broadcasted_iota(jnp.int32, (count, row.shape[-1]), 0)
    return jnp.where(
        at == 0, high, jnp.where(at == 1, low, 0.0)
    ).astype(BF16)


def finish_kernel(recv_ref, rows_ref, encw_ref, gain_ref, embed_ref, send_ref):
    part = rows_ref.shape[0]
    grad = recv_ref[0].astype(F32)
    for s in range(1, recv_ref.shape[0]):
        grad = grad + recv_ref[s].astype(F32)
    raw = rows_ref[...]
    mixed = raw.astype(F32) + mm(raw, encw_ref[...])
    inverse = lax.rsqrt(jnp.mean(mixed * mixed, axis=-1, keepdims=True) + eps_norm)
    normed = mixed * inverse
    gain_part = jnp.sum(grad * normed, axis=0, keepdims=True)
    grad_normed = grad * gain_ref[...]
    grad_mixed = inverse * (
        grad_normed - normed * jnp.mean(grad_normed * normed, axis=-1, keepdims=True)
    )
    grad_low = grad_mixed.astype(BF16)
    embed_ref[...] = (grad_mixed + mm_nt(grad_low, encw_ref[...])).astype(BF16)
    send_ref[pl.ds(0, part), :] = grad_low
    send_ref[pl.ds(part, EXTRA), :] = split_rows(gain_part, EXTRA, lambda v: v.astype(BF16).astype(F32))


def finish(recv, rows, enc_weight, gain):
    part = rows.shape[0]
    return pl.pallas_call(
        finish_kernel,
        out_shape=[
            jax.ShapeDtypeStruct((part, ENC_D), BF16),
            jax.ShapeDtypeStruct((part + EXTRA, ENC_D), BF16),
        ],
        compiler_params=pltpu.CompilerParams(vmem_limit_bytes=40 * 1024 * 1024),
    )(recv, rows, enc_weight, gain)


def add_low(a, b):
    return (a.astype(F32) + b.astype(F32)).astype(BF16)


def add_gain(a, b):
    return (a[0].astype(F32) + a[1].astype(F32)) + (b[0].astype(F32) + b[1].astype(F32))


def body(n_sec, n_dp, nbr_embed, enc_weight, enc_gain, kv_weight, queries, pos_bias, nbr_ids, ctx_grad):
    local_rows = nbr_embed[0].reshape(-1, ENC_D)
    part = local_rows.shape[0]
    gain = enc_gain[None, :]
    rows = lax.all_gather(local_rows, "section", axis=0, tiled=False)
    grad_query, kv_part, grad_enc = layer(
        n_sec, nbr_ids[0], rows, enc_weight, gain, kv_weight[0], queries[0], pos_bias[0], ctx_grad[0]
    )
    kv_grad = lax.psum_scatter(
        kv_part.reshape(-1, ENC_D), "dp", scatter_dimension=0, tiled=True
    ).astype(F32)
    recv = lax.all_to_all(grad_enc, "section", 0, 0, tiled=True)
    embed_grad, send = finish(recv, local_rows, enc_weight, gain)
    got = lax.all_gather(send, "section", axis=0, tiled=False)

    own = ENC_D // n_sec
    mine = lax.dynamic_slice_in_dim(rows, lax.axis_index("section") * own, own, axis=2)
    weight_part = lax.dot_general(
        mine, got[:, :part], (((0, 1), (0, 1)), ((), ())), preferred_element_type=F32
    ).astype(BF16)
    extra = got[:, part:part + 2].astype(F32)
    gain_row = extra[0, 0] + extra[0, 1]
    for s in range(1, n_sec):
        gain_row = gain_row + (extra[s, 0] + extra[s, 1])

    weight_sum = weight_part
    dist = 1
    while dist < n_dp:
        out = jnp.concatenate([weight_sum, split_rows(gain_row[None], EXTRA, lambda v: lax.reduce_precision(v, 8, 7))], axis=0)
        inc = lax.ppermute(out, "dp", [(i, i ^ dist) for i in range(n_dp)])
        weight_sum = add_low(weight_sum, inc[:own])
        gain_row = add_gain(out[own:own + 2], inc[own:own + 2])
        dist *= 2
    return (
        grad_query[None],
        kv_grad[None],
        weight_sum.astype(F32),
        gain_row,
        embed_grad.reshape(nbr_embed.shape),
    )


def solution(mesh):
    return jax.shard_map(
        functools.partial(body, mesh.shape["section"], mesh.shape["dp"]),
        mesh=mesh,
        in_specs=(
            P("dp", None, "section", None),
            P(),
            P(),
            P("section", None, None),
            P("section", "dp", None),
            P("section", None, None, None),
            P("dp", None, None),
            P("section", "dp", None),
        ),
        out_specs=(
            P("section", "dp", None),
            P("section", "dp", None),
            P("section", None),
            P(),
            P("dp", None, "section", None),
        ),
        check_vma=False,
    )
```

```python
import functools
import math

import jax
import jax.numpy as jnp
from jax import lax
from jax.experimental import pallas as pl
from jax.experimental.pallas import tpu as pltpu
from jax.sharding import PartitionSpec as P

HEADS = 16
HEAD = 128
ENC_D = 896
BLOCK = 64
NBR = 2
NLEN = 128
TOK_DEV = 128
NSET = 4
PAIR = 2
STEP = 4
EXTRA = 16

eps_norm = 1e-06
F32 = jnp.float32
BF16 = jnp.bfloat16


def mm(a, b):
    return lax.dot_general(a, b, (((1,), (0,)), ((), ())), preferred_element_type=F32)


def mm_nt(a, b):
    return lax.dot_general(a, b, (((1,), (1,)), ((), ())), preferred_element_type=F32)


def mm_tn(a, b):
    return lax.dot_general(a, b, (((0,), (0,)), ((), ())), preferred_element_type=F32)


def layer_kernel(
    n_sec, ids, rows_ref, encw_ref, gain_ref, w_ref, q_ref, bias_ref, up_ref,
    qg_ref, kvg_ref, ge_ref, enc, proj, total, gset, acc,
):
    step = pl.program_id(0)
    part = NLEN // n_sec
    blocks = TOK_DEV // BLOCK
    width = STEP * HEAD
    factor = 1.0 / math.sqrt(HEAD)

    @pl.when(step == 0)
    def _():
        for s in range(n_sec):
            for e in range(NSET):
                enc[pl.ds(e * NLEN + s * part, part), :] = rows_ref[s, pl.ds(e * part, part), :]
        for e in range(NSET):
            span = pl.ds(e * NLEN, NLEN)
            raw = enc[span, :]
            mixed = raw.astype(F32) + mm(raw, encw_ref[...])
            inverse = lax.rsqrt(jnp.mean(mixed * mixed, axis=-1, keepdims=True) + eps_norm)
            enc[span, :] = ((mixed * inverse) * gain_ref[...]).astype(BF16)
        acc[...] = jnp.zeros_like(acc)

    encoded = enc[...]
    weights = w_ref[...].reshape(2 * width, ENC_D)
    proj[...] = mm_nt(encoded, weights).astype(BF16)
    total[...] = jnp.zeros_like(total)
    spans = [
        [pl.ds(pl.multiple_of(ids[c, n] * NLEN, NLEN), NLEN) for n in range(NBR)]
        for c in range(blocks)
    ]
    toks = [slice(c * BLOCK, (c + 1) * BLOCK) for c in range(blocks)]
    pair = PAIR * HEAD
    items = [(c, g) for c in range(blocks) for g in range(STEP // PAIR)]

    def stacked(ref, c, g):
        x = ref[toks[c], g * pair:(g + 1) * pair]
        head_of = lax.broadcasted_iota(jnp.int32, x.shape, 1) // HEAD
        return jnp.concatenate([jnp.where(head_of == h, x, jnp.zeros_like(x)) for h in range(PAIR)], axis=0)

    def picked(c, g, base):
        return jnp.concatenate([proj[s, base + g * pair:base + (g + 1) * pair] for s in spans[c]], axis=0)

    def bias(g):
        return jnp.concatenate([bias_ref[g * PAIR + h] for h in range(PAIR)], axis=0).astype(F32)

    keys = {i: picked(*i, 0) for i in items}
    values = {i: picked(*i, width) for i in items}
    query = {i: stacked(q_ref, *i) for i in items}
    upstream = {i: stacked(up_ref, *i) for i in items}
    scores = {i: mm_nt(query[i], keys[i]) * factor + bias(i[1]) for i in items}
    dprobs = {i: mm_nt(upstream[i], values[i]) for i in items}
    exps = {i: jnp.exp(scores[i] - jnp.max(scores[i], axis=-1, keepdims=True)) for i in items}
    probs = {i: exps[i] / jnp.sum(exps[i], axis=-1, keepdims=True) for i in items}
    dvalues = {i: mm_tn(probs[i].astype(BF16), upstream[i]) for i in items}
    inner = {i: jnp.sum(probs[i] * dprobs[i], axis=-1, keepdims=True) for i in items}
    dscores = {i: (probs[i] * (dprobs[i] - inner[i])).astype(BF16) for i in items}
    dkeys = {i: mm_tn(dscores[i], query[i]) * factor for i in items}
    dquery = {i: mm(dscores[i], keys[i]) * factor for i in items}
    for c, g in items:
        for h in range(PAIR):
            col = slice(h * HEAD, (h + 1) * HEAD)
            qg_ref[toks[c], g * pair + h * HEAD:g * pair + (h + 1) * HEAD] = (
                dquery[c, g][h * BLOCK:(h + 1) * BLOCK, col].astype(BF16)
            )
        for n, s in enumerate(spans[c]):
            total[s, g * pair:(g + 1) * pair] += dkeys[c, g][n * NLEN:(n + 1) * NLEN]
            total[s, width + g * pair:width + (g + 1) * pair] += dvalues[c, g][n * NLEN:(n + 1) * NLEN]
    gset[...] = total[...].astype(BF16)
    kvg_ref[...] = mm_tn(gset[...], encoded).astype(BF16).reshape(2, width, ENC_D)
    acc[...] += mm(gset[...], weights)

    @pl.when(step == pl.num_programs(0) - 1)
    def _():
        for s in range(n_sec):
            for e in range(NSET):
                ge_ref[s, pl.ds(e * part, part), :] = acc[pl.ds(e * NLEN + s * part, part), :].astype(BF16)


def layer(n_sec, ids, rows, enc_weight, gain, weights, queries, bias, upstream):
    head_width = HEADS * HEAD
    width = STEP * HEAD
    all_rows = NSET * NLEN
    part = all_rows // n_sec
    fixed2 = lambda i, ids: (0, 0)
    fixed3 = lambda i, ids: (0, 0, 0)
    return pl.pallas_call(
        functools.partial(layer_kernel, n_sec),
        grid_spec=pltpu.PrefetchScalarGridSpec(
            num_scalar_prefetch=1,
            grid=(HEADS // STEP,),
            in_specs=[
                pl.BlockSpec((n_sec, part, ENC_D), fixed3),
                pl.BlockSpec((ENC_D, ENC_D), fixed2),
                pl.BlockSpec((1, ENC_D), fixed2),
                pl.BlockSpec((2, width, ENC_D), lambda i, ids: (0, i, 0)),
                pl.BlockSpec((TOK_DEV, width), lambda i, ids: (0, i)),
                pl.BlockSpec((STEP, BLOCK, NBR * NLEN), lambda i, ids: (i, 0, 0)),
                pl.BlockSpec((TOK_DEV, width), lambda i, ids: (0, i)),
            ],
            out_specs=[
                pl.BlockSpec((TOK_DEV, width), lambda i, ids: (0, i)),
                pl.BlockSpec((2, width, ENC_D), lambda i, ids: (0, i, 0)),
                pl.BlockSpec((n_sec, part, ENC_D), fixed3),
            ],
            scratch_shapes=[
                pltpu.VMEM((all_rows, ENC_D), BF16),
                pltpu.VMEM((all_rows, 2 * width), BF16),
                pltpu.VMEM((all_rows, 2 * width), F32),
                pltpu.VMEM((all_rows, 2 * width), BF16),
                pltpu.VMEM((all_rows, ENC_D), F32),
            ],
        ),
        out_shape=[
            jax.ShapeDtypeStruct((TOK_DEV, head_width), BF16),
            jax.ShapeDtypeStruct((2, head_width, ENC_D), BF16),
            jax.ShapeDtypeStruct((n_sec, part, ENC_D), BF16),
        ],
        compiler_params=pltpu.CompilerParams(
            vmem_limit_bytes=60 * 1024 * 1024, dimension_semantics=("arbitrary",)
        ),
    )(ids, rows, enc_weight, gain, weights.reshape(2, head_width, ENC_D), queries, bias, upstream)


def split_rows(row, count, rounded):
    high = rounded(row)
    low = row - high
    at = lax.broadcasted_iota(jnp.int32, (count, row.shape[-1]), 0)
    return jnp.where(
        at == 0, high, jnp.where(at == 1, low, 0.0)
    ).astype(BF16)


def finish_kernel(recv_ref, rows_ref, encw_ref, gain_ref, embed_ref, send_ref):
    part = rows_ref.shape[0]
    grad = recv_ref[0].astype(F32)
    for s in range(1, recv_ref.shape[0]):
        grad = grad + recv_ref[s].astype(F32)
    raw = rows_ref[...]
    mixed = raw.astype(F32) + mm(raw, encw_ref[...])
    inverse = lax.rsqrt(jnp.mean(mixed * mixed, axis=-1, keepdims=True) + eps_norm)
    normed = mixed * inverse
    gain_part = jnp.sum(grad * normed, axis=0, keepdims=True)
    grad_normed = grad * gain_ref[...]
    grad_mixed = inverse * (
        grad_normed - normed * jnp.mean(grad_normed * normed, axis=-1, keepdims=True)
    )
    grad_low = grad_mixed.astype(BF16)
    embed_ref[...] = (grad_mixed + mm_nt(grad_low, encw_ref[...])).astype(BF16)
    send_ref[pl.ds(0, part), :] = grad_low
    send_ref[pl.ds(part, EXTRA), :] = split_rows(gain_part, EXTRA, lambda v: v.astype(BF16).astype(F32))


def finish(recv, rows, enc_weight, gain):
    part = rows.shape[0]
    return pl.pallas_call(
        finish_kernel,
        out_shape=[
            jax.ShapeDtypeStruct((part, ENC_D), BF16),
            jax.ShapeDtypeStruct((part + EXTRA, ENC_D), BF16),
        ],
        compiler_params=pltpu.CompilerParams(vmem_limit_bytes=60 * 1024 * 1024),
    )(recv, rows, enc_weight, gain)


def add_low(a, b):
    return (a.astype(F32) + b.astype(F32)).astype(BF16)


def add_gain(a, b):
    return (a[0].astype(F32) + a[1].astype(F32)) + (b[0].astype(F32) + b[1].astype(F32))


def body(n_sec, n_dp, nbr_embed, enc_weight, enc_gain, kv_weight, queries, pos_bias, nbr_ids, ctx_grad):
    local_rows = nbr_embed[0].reshape(-1, ENC_D)
    part = local_rows.shape[0]
    gain = enc_gain[None, :]
    rows = lax.all_gather(local_rows, "section", axis=0, tiled=False)
    grad_query, kv_part, grad_enc = layer(
        n_sec, nbr_ids[0], rows, enc_weight, gain, kv_weight[0], queries[0], pos_bias[0], ctx_grad[0]
    )
    kv_grad = lax.psum_scatter(
        kv_part.reshape(-1, ENC_D), "dp", scatter_dimension=0, tiled=True
    ).astype(F32)
    recv = lax.all_to_all(grad_enc, "section", 0, 0, tiled=True)
    embed_grad, send = finish(recv, local_rows, enc_weight, gain)
    got = lax.all_gather(send, "section", axis=0, tiled=False)

    own = ENC_D // n_sec
    mine = lax.dynamic_slice_in_dim(rows, lax.axis_index("section") * own, own, axis=2)
    weight_part = lax.dot_general(
        mine, got[:, :part], (((0, 1), (0, 1)), ((), ())), preferred_element_type=F32
    ).astype(BF16)
    extra = got[:, part:part + 2].astype(F32)
    gain_row = extra[0, 0] + extra[0, 1]
    for s in range(1, n_sec):
        gain_row = gain_row + (extra[s, 0] + extra[s, 1])

    rank = lax.axis_index("dp")
    half = own // 2
    odd = lax.rem(rank, 2)
    near = [(i, i ^ 1) for i in range(n_dp)]
    extra_rows = split_rows(gain_row[None], EXTRA, lambda v: lax.reduce_precision(v, 8, 7))
    kept = lax.dynamic_slice_in_dim(weight_part, odd * half, half, axis=0)
    given = lax.dynamic_slice_in_dim(weight_part, (1 - odd) * half, half, axis=0)
    inc = lax.ppermute(jnp.concatenate([given, extra_rows], axis=0), "dp", near)
    weight_sum = add_low(kept, inc[:half])
    gain_row = add_gain(extra_rows, inc[half:half + 2])
    dist = 2
    while dist < n_dp:
        out = jnp.concatenate([weight_sum, split_rows(gain_row[None], EXTRA, lambda v: lax.reduce_precision(v, 8, 7))], axis=0)
        inc = lax.ppermute(out, "dp", [(i, i ^ dist) for i in range(n_dp)])
        weight_sum = add_low(weight_sum, inc[:half])
        gain_row = add_gain(out[half:half + 2], inc[half:half + 2])
        dist *= 2
    inc = lax.ppermute(weight_sum, "dp", near)
    weight_sum = jnp.where(
        odd == 0,
        jnp.concatenate([weight_sum, inc], axis=0),
        jnp.concatenate([inc, weight_sum], axis=0),
    )
    return (
        grad_query[None],
        kv_grad[None],
        weight_sum.astype(F32),
        gain_row,
        embed_grad.reshape(nbr_embed.shape),
    )


def solution(mesh):
    return jax.shard_map(
        functools.partial(body, mesh.shape["section"], mesh.shape["dp"]),
        mesh=mesh,
        in_specs=(
            P("dp", None, "section", None),
            P(),
            P(),
            P("section", None, None),
            P("section", "dp", None),
            P("section", None, None, None),
            P("dp", None, None),
            P("section", "dp", None),
        ),
        out_specs=(
            P("section", "dp", None),
            P("section", "dp", None),
            P("section", None),
            P(),
            P("dp", None, "section", None),
        ),
        check_vma=False,
    )
```

```python
import functools
import math

import jax
import jax.numpy as jnp
from jax import lax
from jax.experimental import pallas as pl
from jax.experimental.pallas import tpu as pltpu
from jax.sharding import PartitionSpec as P

HEADS = 16
HEAD = 128
ENC_D = 896
BLOCK = 64
NBR = 2
NLEN = 128
TOK_DEV = 128
NSET = 4
PAIR = 2
STEP = 4
EXTRA = 16

eps_norm = 1e-06
LIMIT = 60 * 1024 * 1024
F32 = jnp.float32
BF16 = jnp.bfloat16


def mm(a, b):
    return lax.dot_general(a, b, (((1,), (0,)), ((), ())), preferred_element_type=F32)


def mm_nt(a, b):
    return lax.dot_general(a, b, (((1,), (1,)), ((), ())), preferred_element_type=F32)


def mm_tn(a, b):
    return lax.dot_general(a, b, (((0,), (0,)), ((), ())), preferred_element_type=F32)


def layer_kernel(
    n_sec, ids, me, rows_ref, encw_ref, gain_ref, w_ref, q_ref, bias_ref, up_ref, qg_ref, kvg_ref, *rest,
):
    ge_refs, (enc, proj, total, gset, acc) = rest[:n_sec], rest[n_sec:]
    step = pl.program_id(0)
    part = NLEN // n_sec
    blocks = TOK_DEV // BLOCK
    width = STEP * HEAD
    factor = 1.0 / math.sqrt(HEAD)

    @pl.when(step == 0)
    def _():
        for s in range(n_sec):
            for e in range(NSET):
                enc[pl.ds(e * NLEN + s * part, part), :] = rows_ref[s, pl.ds(e * part, part), :]
        for e in range(NSET):
            span = pl.ds(e * NLEN, NLEN)
            raw = enc[span, :]
            mixed = raw.astype(F32) + mm(raw, encw_ref[...])
            inverse = lax.rsqrt(jnp.mean(mixed * mixed, axis=-1, keepdims=True) + eps_norm)
            enc[span, :] = ((mixed * inverse) * gain_ref[...]).astype(BF16)
        acc[...] = jnp.zeros_like(acc)

    encoded = enc[...]
    weights = w_ref[...].reshape(2 * width, ENC_D)
    proj[...] = mm_nt(encoded, weights).astype(BF16)
    total[...] = jnp.zeros_like(total)
    spans = [
        [pl.ds(pl.multiple_of(ids[c, n] * NLEN, NLEN), NLEN) for n in range(NBR)]
        for c in range(blocks)
    ]
    toks = [slice(c * BLOCK, (c + 1) * BLOCK) for c in range(blocks)]
    pair = PAIR * HEAD
    items = [(c, g) for c in range(blocks) for g in range(STEP // PAIR)]

    def stacked(ref, c, g):
        x = ref[toks[c], g * pair:(g + 1) * pair]
        head_of = lax.broadcasted_iota(jnp.int32, x.shape, 1) // HEAD
        return jnp.concatenate([jnp.where(head_of == h, x, jnp.zeros_like(x)) for h in range(PAIR)], axis=0)

    def picked(c, g, base):
        return jnp.concatenate([proj[s, base + g * pair:base + (g + 1) * pair] for s in spans[c]], axis=0)

    def bias(g):
        return jnp.concatenate([bias_ref[g * PAIR + h] for h in range(PAIR)], axis=0).astype(F32)

    keys = {i: picked(*i, 0) for i in items}
    values = {i: picked(*i, width) for i in items}
    query = {i: stacked(q_ref, *i) for i in items}
    upstream = {i: stacked(up_ref, *i) for i in items}
    scores = {i: mm_nt(query[i], keys[i]) * factor + bias(i[1]) for i in items}
    dprobs = {i: mm_nt(upstream[i], values[i]) for i in items}
    exps = {i: jnp.exp(scores[i] - jnp.max(scores[i], axis=-1, keepdims=True)) for i in items}
    probs = {i: exps[i] / jnp.sum(exps[i], axis=-1, keepdims=True) for i in items}
    dvalues = {i: mm_tn(probs[i].astype(BF16), upstream[i]) for i in items}
    inner = {i: jnp.sum(probs[i] * dprobs[i], axis=-1, keepdims=True) for i in items}
    dscores = {i: (probs[i] * (dprobs[i] - inner[i])).astype(BF16) for i in items}
    dkeys = {i: mm_tn(dscores[i], query[i]) * factor for i in items}
    dquery = {i: mm(dscores[i], keys[i]) * factor for i in items}
    for c, g in items:
        for h in range(PAIR):
            col = slice(h * HEAD, (h + 1) * HEAD)
            qg_ref[toks[c], g * pair + h * HEAD:g * pair + (h + 1) * HEAD] = (
                dquery[c, g][h * BLOCK:(h + 1) * BLOCK, col].astype(BF16)
            )
        for n, s in enumerate(spans[c]):
            total[s, g * pair:(g + 1) * pair] += dkeys[c, g][n * NLEN:(n + 1) * NLEN]
            total[s, width + g * pair:width + (g + 1) * pair] += dvalues[c, g][n * NLEN:(n + 1) * NLEN]
    gset[...] = total[...].astype(BF16)
    kvg_ref[...] = mm_tn(gset[...], encoded).astype(BF16).reshape(2, width, ENC_D)
    acc[...] += mm(gset[...], weights)

    @pl.when(step == pl.num_programs(0) - 1)
    def _():
        for k in range(n_sec):
            s = lax.rem(me[0] + k, n_sec)
            for e in range(NSET):
                span = pl.ds(pl.multiple_of(e * NLEN + s * part, part), part)
                ge_refs[k][pl.ds(e * part, part), :] = acc[span, :].astype(BF16)


def layer(n_sec, ids, me, rows, enc_weight, gain, weights, queries, bias, upstream):
    head_width = HEADS * HEAD
    width = STEP * HEAD
    all_rows = NSET * NLEN
    part = all_rows // n_sec
    fixed2 = lambda i, *_: (0, 0)
    fixed3 = lambda i, *_: (0, 0, 0)
    return pl.pallas_call(
        functools.partial(layer_kernel, n_sec),
        grid_spec=pltpu.PrefetchScalarGridSpec(
            num_scalar_prefetch=2,
            grid=(HEADS // STEP,),
            in_specs=[
                pl.BlockSpec((n_sec, part, ENC_D), fixed3),
                pl.BlockSpec((ENC_D, ENC_D), fixed2),
                pl.BlockSpec((1, ENC_D), fixed2),
                pl.BlockSpec((2, width, ENC_D), lambda i, *_: (0, i, 0)),
                pl.BlockSpec((TOK_DEV, width), lambda i, *_: (0, i)),
                pl.BlockSpec((STEP, BLOCK, NBR * NLEN), lambda i, *_: (i, 0, 0)),
                pl.BlockSpec((TOK_DEV, width), lambda i, *_: (0, i)),
            ],
            out_specs=[
                pl.BlockSpec((TOK_DEV, width), lambda i, *_: (0, i)),
                pl.BlockSpec((2, width, ENC_D), lambda i, *_: (0, i, 0)),
            ]
            + [pl.BlockSpec((part, ENC_D), fixed2)] * n_sec,
            scratch_shapes=[
                pltpu.VMEM((all_rows, ENC_D), BF16),
                pltpu.VMEM((all_rows, 2 * width), BF16),
                pltpu.VMEM((all_rows, 2 * width), F32),
                pltpu.VMEM((all_rows, 2 * width), BF16),
                pltpu.VMEM((all_rows, ENC_D), F32),
            ],
        ),
        out_shape=[
            jax.ShapeDtypeStruct((TOK_DEV, head_width), BF16),
            jax.ShapeDtypeStruct((2, head_width, ENC_D), BF16),
        ]
        + [jax.ShapeDtypeStruct((part, ENC_D), BF16)] * n_sec,
        compiler_params=pltpu.CompilerParams(
            vmem_limit_bytes=LIMIT, dimension_semantics=("arbitrary",)
        ),
    )(ids, me, rows, enc_weight, gain, weights.reshape(2, head_width, ENC_D), queries, bias, upstream)


def call(kernel, outs, *args, **kw):
    return pl.pallas_call(
        kernel,
        out_shape=[jax.ShapeDtypeStruct(shape, dtype) for shape, dtype in outs],
        compiler_params=pltpu.CompilerParams(vmem_limit_bytes=LIMIT),
        **kw,
    )(*args)


def split_rows(row):
    high = row.astype(BF16).astype(F32)
    at = lax.broadcasted_iota(jnp.int32, (EXTRA, row.shape[-1]), 0)
    return jnp.where(at == 0, high, jnp.where(at == 1, row - high, 0.0)).astype(BF16)


def joined(ref):
    extra = ref[pl.ds(0, EXTRA), :].astype(F32)
    return extra[0:1] + extra[1:2]


def finish_kernel(*refs):
    *grads, rows_ref, encw_ref, gain_ref, embed_ref, send_ref = refs
    grad = grads[0][...].astype(F32)
    for g in grads[1:]:
        grad = grad + g[...].astype(F32)
    raw = rows_ref[...]
    mixed = raw.astype(F32) + mm(raw, encw_ref[...])
    inverse = lax.rsqrt(jnp.mean(mixed * mixed, axis=-1, keepdims=True) + eps_norm)
    normed = mixed * inverse
    gain_part = jnp.sum(grad * normed, axis=0, keepdims=True)
    grad_normed = grad * gain_ref[...]
    grad_mixed = inverse * (
        grad_normed - normed * jnp.mean(grad_normed * normed, axis=-1, keepdims=True)
    )
    grad_low = grad_mixed.astype(BF16)
    embed_ref[...] = (grad_mixed + mm_nt(grad_low, encw_ref[...])).astype(BF16)
    send_ref[pl.ds(0, EXTRA), :] = split_rows(gain_part)
    send_ref[pl.ds(EXTRA, raw.shape[0]), :] = grad_low


def outer_kernel(n_sec, where, mine_ref, *refs):
    *gots, keep_ref, give_ref, total = refs
    me, odd = where[0], where[1]
    part = mine_ref.shape[1]
    half = keep_ref.shape[0]
    full = mm_tn(mine_ref[0], gots[0][pl.ds(EXTRA, part), :])
    for k in range(1, n_sec):
        full = full + mm_tn(mine_ref[k], gots[k][pl.ds(EXTRA, part), :])
    total[...] = full
    keep_ref[...] = total[pl.ds(pl.multiple_of(odd * half, 8), half), :].astype(BF16)
    give_ref[pl.ds(EXTRA, half), :] = total[pl.ds(pl.multiple_of((1 - odd) * half, 8), half), :].astype(BF16)
    rows = [joined(g) for g in gots]
    gain_row = jnp.zeros_like(rows[0])
    for s in range(n_sec):
        for k in range(n_sec):
            here = lax.rem(me + n_sec - k, n_sec) == s
            gain_row = gain_row + jnp.where(here, rows[k], 0.0)
    give_ref[pl.ds(0, EXTRA), :] = split_rows(gain_row)


def first_merge_kernel(keep_ref, give_ref, inc_ref, out_ref):
    half = keep_ref.shape[0]
    out_ref[pl.ds(0, EXTRA), :] = split_rows(joined(give_ref) + joined(inc_ref))
    out_ref[pl.ds(EXTRA, half), :] = (
        keep_ref[...].astype(F32) + inc_ref[pl.ds(EXTRA, half), :].astype(F32)
    ).astype(BF16)


def merge_kernel(own_ref, inc_ref, out_ref):
    half = own_ref.shape[0] - EXTRA
    out_ref[pl.ds(0, EXTRA), :] = split_rows(joined(own_ref) + joined(inc_ref))
    out_ref[pl.ds(EXTRA, half), :] = (
        own_ref[pl.ds(EXTRA, half), :].astype(F32) + inc_ref[pl.ds(EXTRA, half), :].astype(F32)
    ).astype(BF16)


def spread_kernel(where, own_ref, inc_ref, weight_ref, gain_ref):
    half = own_ref.shape[0] - EXTRA
    odd = where[1]
    weight_ref[pl.ds(pl.multiple_of(odd * half, 8), half), :] = own_ref[pl.ds(EXTRA, half), :].astype(F32)
    weight_ref[pl.ds(pl.multiple_of((1 - odd) * half, 8), half), :] = inc_ref[pl.ds(EXTRA, half), :].astype(F32)
    gain_ref[...] = joined(own_ref)


def sum_kernel(at, *refs):
    *ins, out_ref = refs
    total = ins[0][...].astype(F32)
    for r in ins[1:]:
        total = total + r[...].astype(F32)
    out_ref[...] = total.astype(out_ref.dtype)


def block_sum(rows, dtype, *terms):
    cut = 2 if rows % 32 == 0 else 1
    size = rows // cut
    arrays = [a for a, _ in terms]
    at = jnp.stack([jnp.asarray(i, jnp.int32) for _, i in terms])
    spec = lambda n: pl.BlockSpec((size, ENC_D), lambda i, at: (at[n] * cut + i, 0))
    return pl.pallas_call(
        sum_kernel,
        grid_spec=pltpu.PrefetchScalarGridSpec(
            num_scalar_prefetch=1,
            grid=(cut,),
            in_specs=[spec(n) for n in range(len(terms))],
            out_specs=pl.BlockSpec((size, ENC_D), lambda i, at: (i, 0)),
        ),
        out_shape=jax.ShapeDtypeStruct((rows, ENC_D), dtype),
        compiler_params=pltpu.CompilerParams(vmem_limit_bytes=LIMIT),
        cost_estimate=pl.CostEstimate(
            flops=rows * ENC_D * len(terms), bytes_accessed=2 * rows * ENC_D * (len(terms) + 1), transcendentals=0
        ),
    )(at, *arrays)


def chip_sum(n_dp, parts):
    rows = parts.shape[0] // n_dp
    chips = n_dp // 2
    near = [(i, i ^ 1) for i in range(n_dp)]
    rank = lax.axis_index("dp")
    chip, core = rank // 2, lax.rem(rank, 2)

    def chunk(step, of_core):
        place = jnp.where(of_core == 0, chip, chips - 1 - chip)
        ahead = jnp.minimum(chips - step + place, chips - 1)
        return jnp.where(of_core == 0, ahead, chips - 1 - ahead)

    incoming = [None, None]
    for step in range(1, chips):
        theirs = lax.dynamic_slice_in_dim(parts, chunk(step, 1 - core) * 2 * rows, 2 * rows, axis=0)
        ours = lax.ppermute(theirs, "dp", near)
        hops = [(2 * a, 2 * a + 2) for a in range(step)]
        hops += [(2 * (chips - 1 - a) + 1, 2 * (chips - 2 - a) + 1) for a in range(step)]
        for j in range(2):
            lane = jnp.where(j == 0, 1 - core, core)
            terms = [(parts, 2 * chunk(step, core) + lane), (ours, lane)]
            if incoming[j] is not None:
                terms.append((incoming[j], 0))
            incoming[j] = lax.ppermute(block_sum(rows, BF16, *terms), "dp", hops)
    other = block_sum(rows, BF16, (parts, rank + 1 - 2 * core), *([(incoming[0], 0)] if chips > 1 else []))
    swapped = lax.ppermute(other, "dp", near)
    return block_sum(rows, F32, (parts, rank), (swapped, 0), *([(incoming[1], 0)] if chips > 1 else []))


def rotated(x, n, k):
    return lax.ppermute(x, "section", [(i, (i + k) % n) for i in range(n)]) if k else x


def body(n_sec, n_dp, nbr_embed, enc_weight, enc_gain, kv_weight, queries, pos_bias, nbr_ids, ctx_grad):
    local_rows = nbr_embed[0].reshape(-1, ENC_D)
    part = local_rows.shape[0]
    own = ENC_D // n_sec
    half = own // 2
    gain = enc_gain[None, :]
    me = lax.axis_index("section")
    rank = lax.axis_index("dp")
    where = jnp.stack([me, lax.rem(rank, 2)]).astype(jnp.int32)
    rows = lax.all_gather(local_rows, "section", axis=0, tiled=False)
    mine = lax.dynamic_slice_in_dim(rows, me * own, own, axis=2)
    mine = jnp.stack([lax.dynamic_index_in_dim(mine, lax.rem(me + n_sec - k, n_sec), 0, False) for k in range(n_sec)])
    grad_query, kv_part, *grad_enc = layer(
        n_sec, nbr_ids[0], where, rows, enc_weight, gain, kv_weight[0], queries[0], pos_bias[0], ctx_grad[0]
    )
    got = [rotated(grad_enc[k], n_sec, k) for k in range(n_sec)]
    kv_grad = chip_sum(n_dp, kv_part.reshape(-1, ENC_D))
    embed_grad, send = call(
        finish_kernel,
        [((part, ENC_D), BF16), ((EXTRA + part, ENC_D), BF16)],
        *got, local_rows, enc_weight, gain,
    )
    lows = [rotated(send, n_sec, k) for k in range(n_sec)]
    vmem = pl.BlockSpec(memory_space=pltpu.VMEM)
    smem = pl.BlockSpec(memory_space=pltpu.SMEM)
    keep, give = call(
        functools.partial(outer_kernel, n_sec),
        [((half, ENC_D), BF16), ((EXTRA + half, ENC_D), BF16)],
        where, mine, *lows,
        in_specs=[smem] + [vmem] * (1 + n_sec),
        scratch_shapes=[pltpu.VMEM((own, ENC_D), F32)],
    )
    swap = lambda x, dist: lax.ppermute(x, "dp", [(i, i ^ dist) for i in range(n_dp)])
    shape = [((EXTRA + half, ENC_D), BF16)]
    (weight_sum,) = call(first_merge_kernel, shape, keep, give, swap(give, 1))
    dist = 2
    while dist < n_dp:
        (weight_sum,) = call(merge_kernel, shape, weight_sum, swap(weight_sum, dist))
        dist *= 2
    weight_grad, gain_row = call(
        spread_kernel, [((own, ENC_D), F32), ((1, ENC_D), F32)], where, weight_sum, swap(weight_sum, 1),
        in_specs=[smem] + [vmem] * 2,
    )
    return (
        grad_query[None],
        kv_grad[None],
        weight_grad,
        gain_row[0],
        embed_grad.reshape(nbr_embed.shape),
    )


def solution(mesh):
    return jax.shard_map(
        functools.partial(body, mesh.shape["section"], mesh.shape["dp"]),
        mesh=mesh,
        in_specs=(
            P("dp", None, "section", None),
            P(),
            P(),
            P("section", None, None),
            P("section", "dp", None),
            P("section", None, None, None),
            P("dp", None, None),
            P("section", "dp", None),
        ),
        out_specs=(
            P("section", "dp", None),
            P("section", "dp", None),
            P("section", None),
            P(),
            P("dp", None, "section", None),
        ),
        check_vma=False,
    )
```

```python
import functools
import math

import jax
import jax.numpy as jnp
from jax import lax
from jax.experimental import pallas as pl
from jax.experimental.pallas import tpu as pltpu
from jax.sharding import PartitionSpec as P

HEADS = 16
HEAD = 128
ENC_D = 896
BLOCK = 64
NBR = 2
NLEN = 128
TOK_DEV = 128
NSET = 4
PAIR = 2
STEP = 4
EXTRA = 16

eps_norm = 1e-06
LIMIT = 65400 * 1024
SHORT = pl.CostEstimate(flops=1, bytes_accessed=1, transcendentals=0)
LONGER = pl.CostEstimate(flops=20_000_000_000, bytes_accessed=20_000_000, transcendentals=0)
F32 = jnp.float32
BF16 = jnp.bfloat16


def mm(a, b):
    return lax.dot_general(a, b, (((1,), (0,)), ((), ())), preferred_element_type=F32)


def mm_nt(a, b):
    return lax.dot_general(a, b, (((1,), (1,)), ((), ())), preferred_element_type=F32)


def mm_tn(a, b):
    return lax.dot_general(a, b, (((0,), (0,)), ((), ())), preferred_element_type=F32)


def blocks_of(n_give, width):
    return max(1, 2 * HEADS * HEAD // (n_give + 1) // width)


def normalised(raw, encw_ref):
    mixed = raw.astype(F32) + mm(raw, encw_ref[...])
    inverse = lax.rsqrt(jnp.mean(mixed * mixed, axis=-1, keepdims=True) + eps_norm)
    return mixed * inverse, inverse


def layer_kernel(
    n_sec, n_give, ids, where, rows_ref, encw_ref, gain_ref, w_ref, q_ref, bias_ref, up_ref,
    qg_ref, kvg_ref, normed_ref, inverse_ref, *rest,
):
    n_arrays = min(n_give, 2)
    ge_refs, give_refs = rest[:n_sec], rest[n_sec:n_sec + n_arrays]
    enc, proj, total, gset, acc = rest[n_sec + n_arrays:]
    step = pl.program_id(0)
    part = NLEN // n_sec
    blocks = TOK_DEV // BLOCK
    width = STEP * HEAD
    factor = 1.0 / math.sqrt(HEAD)

    @pl.when(step == 0)
    def _():
        for s in range(n_sec):
            for e in range(NSET):
                enc[pl.ds(e * NLEN + s * part, part), :] = rows_ref[s, pl.ds(e * part, part), :]
        normed, _ = normalised(enc[...], encw_ref)
        enc[...] = (normed * gain_ref[...][None, :]).astype(BF16)
        normed, inverse = normalised(rows_ref[where[0]], encw_ref)
        normed_ref[...] = normed
        inverse_ref[...] = jnp.broadcast_to(inverse, inverse_ref.shape)
        acc[...] = jnp.zeros_like(acc)

    encoded = enc[...]
    weights = w_ref[...].reshape(2 * width, ENC_D)
    proj[...] = mm_nt(encoded, weights).astype(BF16)
    total[...] = jnp.zeros_like(total)
    spans = [
        [pl.ds(pl.multiple_of(ids[c, n] * NLEN, NLEN), NLEN) for n in range(NBR)]
        for c in range(blocks)
    ]
    toks = [slice(c * BLOCK, (c + 1) * BLOCK) for c in range(blocks)]
    pair = PAIR * HEAD
    items = [(c, g) for c in range(blocks) for g in range(STEP // PAIR)]

    def stacked(ref, c, g):
        x = ref[toks[c], g * pair:(g + 1) * pair]
        head_of = lax.broadcasted_iota(jnp.int32, x.shape, 1) // HEAD
        return jnp.concatenate([jnp.where(head_of == h, x, jnp.zeros_like(x)) for h in range(PAIR)], axis=0)

    def picked(c, g, base):
        return jnp.concatenate([proj[s, base + g * pair:base + (g + 1) * pair] for s in spans[c]], axis=0)

    def bias(g):
        return jnp.concatenate([bias_ref[g * PAIR + h] for h in range(PAIR)], axis=0).astype(F32)

    keys = {i: picked(*i, 0) for i in items}
    values = {i: picked(*i, width) for i in items}
    query = {i: stacked(q_ref, *i) for i in items}
    upstream = {i: stacked(up_ref, *i) for i in items}
    scores = {i: mm_nt(query[i], keys[i]) * factor + bias(i[1]) for i in items}
    dprobs = {i: mm_nt(upstream[i], values[i]) for i in items}
    exps = {i: jnp.exp(scores[i] - jnp.max(scores[i], axis=-1, keepdims=True)) for i in items}
    probs = {i: exps[i] / jnp.sum(exps[i], axis=-1, keepdims=True) for i in items}
    dvalues = {i: mm_tn(probs[i].astype(BF16), upstream[i]) for i in items}
    inner = {i: jnp.sum(probs[i] * dprobs[i], axis=-1, keepdims=True) for i in items}
    dscores = {i: (probs[i] * (dprobs[i] - inner[i])).astype(BF16) for i in items}
    dkeys = {i: mm_tn(dscores[i], query[i]) * factor for i in items}
    dquery = {i: mm(dscores[i], keys[i]) * factor for i in items}
    for c, g in items:
        for h in range(PAIR):
            col = slice(h * HEAD, (h + 1) * HEAD)
            qg_ref[toks[c], g * pair + h * HEAD:g * pair + (h + 1) * HEAD] = (
                dquery[c, g][h * BLOCK:(h + 1) * BLOCK, col].astype(BF16)
            )
        for n, s in enumerate(spans[c]):
            total[s, g * pair:(g + 1) * pair] += dkeys[c, g][n * NLEN:(n + 1) * NLEN]
            total[s, width + g * pair:width + (g + 1) * pair] += dvalues[c, g][n * NLEN:(n + 1) * NLEN]
    gset[...] = total[...].astype(BF16)
    acc[...] += mm(gset[...], weights)
    kvg_ref[...] = mm_tn(gset[...], encoded).astype(BF16).reshape(kvg_ref.shape)
    count = blocks_of(n_give, width)
    for t in range(n_give):
        first, kind, offset = (where[2 + 3 * t + n] for n in range(3))
        size = give_refs[0].shape[0]

        @pl.when((step >= first) & (step < first + count))
        def _():
            block = kvg_ref[kind, pl.ds(pl.multiple_of(offset, size), size), :]
            if t == 0:
                give_refs[0][...] = block
            else:
                at = ((t - 1) * count + step - first) * size
                give_refs[1][pl.ds(pl.multiple_of(at, size), size), :] = block

    @pl.when(step == pl.num_programs(0) - 1)
    def _():
        for k in range(n_sec):
            s = lax.rem(where[0] + k, n_sec)
            for e in range(NSET):
                span = pl.ds(pl.multiple_of(e * NLEN + s * part, part), part)
                ge_refs[k][pl.ds(e * part, part), :] = acc[span, :].astype(BF16)


def layer(n_sec, n_give, ids, where, rows, enc_weight, gain, weights, queries, bias, upstream):
    head_width = HEADS * HEAD
    width = STEP * HEAD
    steps = HEADS // STEP
    all_rows = NSET * NLEN
    part = all_rows // n_sec
    chunk = 2 * head_width // (n_give + 1)
    count = blocks_of(n_give, width)

    def give_specs():
        at = lambda i, ids, where: (jnp.clip(i - where[2], 0, count - 1), 0)
        return [pl.BlockSpec((min(width, chunk), ENC_D), at), pl.BlockSpec((chunk * (n_give - 1), ENC_D), fixed2)]

    fixed2 = lambda i, *_: (0, 0)
    fixed3 = lambda i, *_: (0, 0, 0)
    return pl.pallas_call(
        functools.partial(layer_kernel, n_sec, n_give),
        grid_spec=pltpu.PrefetchScalarGridSpec(
            num_scalar_prefetch=2,
            grid=(steps,),
            in_specs=[
                pl.BlockSpec((n_sec, part, ENC_D), fixed3),
                pl.BlockSpec((ENC_D, ENC_D), fixed2),
                pl.BlockSpec((ENC_D,), lambda i, *_: (0,)),
                pl.BlockSpec((2, width, ENC_D), lambda i, *_: (0, i, 0)),
                pl.BlockSpec((TOK_DEV, width), lambda i, *_: (0, i)),
                pl.BlockSpec((STEP, BLOCK, NBR * NLEN), lambda i, *_: (i, 0, 0)),
                pl.BlockSpec((TOK_DEV, width), lambda i, *_: (0, i)),
            ],
            out_specs=[
                pl.BlockSpec((TOK_DEV, width), lambda i, *_: (0, i)),
                pl.BlockSpec((2, width, ENC_D), lambda i, *_: (0, i, 0)),
                pl.BlockSpec((part, ENC_D), fixed2),
                pl.BlockSpec((part, HEAD), fixed2),
            ]
            + [pl.BlockSpec((part, ENC_D), fixed2)] * n_sec
            + give_specs()[:n_give],
            scratch_shapes=[
                pltpu.VMEM((all_rows, ENC_D), BF16),
                pltpu.VMEM((all_rows, 2 * width), BF16),
                pltpu.VMEM((all_rows, 2 * width), F32),
                pltpu.VMEM((all_rows, 2 * width), BF16),
                pltpu.VMEM((all_rows, ENC_D), F32),
            ],
        ),
        out_shape=[
            jax.ShapeDtypeStruct((TOK_DEV, head_width), BF16),
            jax.ShapeDtypeStruct((2, head_width, ENC_D), BF16),
            jax.ShapeDtypeStruct((part, ENC_D), F32),
            jax.ShapeDtypeStruct((part, HEAD), F32),
        ]
        + [jax.ShapeDtypeStruct((part, ENC_D), BF16)] * n_sec
        + [jax.ShapeDtypeStruct((chunk * n, ENC_D), BF16) for n in (1, n_give - 1)][:n_give],
        compiler_params=pltpu.CompilerParams(
            vmem_limit_bytes=LIMIT, dimension_semantics=("arbitrary",)
        ),
        cost_estimate=SHORT,
    )(ids, where, rows, enc_weight, gain, weights.reshape(2, head_width, ENC_D), queries, bias, upstream)


def call(kernel, outs, *args, after=(), carry=(), scalars=0, scratch_shapes=()):
    n_in, n_out, n_extra, n_carry = len(args), len(outs), len(after), len(carry)

    def inner(*refs):
        own = refs[n_in + n_extra + n_carry:]
        kernel(*refs[:n_in], *own[:n_out], *own[n_out + n_carry:])

    vmem, anywhere = pl.BlockSpec(memory_space=pltpu.VMEM), pl.BlockSpec(memory_space=pl.ANY)
    return pl.pallas_call(
        inner,
        in_specs=[pl.BlockSpec(memory_space=pltpu.SMEM)] * scalars
        + [vmem] * (n_in - scalars)
        + [anywhere] * (n_extra + n_carry),
        out_specs=[vmem] * n_out + [anywhere] * n_carry,
        out_shape=[jax.ShapeDtypeStruct(shape, dtype) for shape, dtype in outs]
        + [jax.ShapeDtypeStruct(x.shape, x.dtype) for x in carry],
        input_output_aliases={n_in + n_extra + k: n_out + k for k in range(n_carry)},
        scratch_shapes=scratch_shapes,
        compiler_params=pltpu.CompilerParams(vmem_limit_bytes=LIMIT),
        cost_estimate=LONGER,
    )(*args, *after, *carry)


def split_rows(row):
    high = row.astype(BF16).astype(F32)
    at = lax.broadcasted_iota(jnp.int32, (EXTRA, row.shape[-1]), 0)
    return jnp.where(at == 0, high, jnp.where(at == 1, row - high, 0.0)).astype(BF16)


def joined(ref):
    extra = ref[pl.ds(0, EXTRA), :].astype(F32)
    return extra[0:1] + extra[1:2]


def finish_kernel(*refs):
    *grads, normed_ref, inverse_ref, gain_ref, mixed_ref, send_ref = refs
    grad = grads[0][...].astype(F32)
    for g in grads[1:]:
        grad = grad + g[...].astype(F32)
    normed = normed_ref[...]
    grad_normed = grad * gain_ref[...][None, :]
    grad_mixed = inverse_ref[...][:, :1] * (
        grad_normed - normed * jnp.mean(grad_normed * normed, axis=-1, keepdims=True)
    )
    mixed_ref[...] = grad_mixed
    send_ref[pl.ds(0, EXTRA), :] = split_rows(jnp.sum(grad * normed, axis=0, keepdims=True))
    send_ref[pl.ds(EXTRA, normed.shape[0]), :] = grad_mixed.astype(BF16)


def embed_kernel(mixed_ref, encw_ref, embed_ref):
    grad_mixed = mixed_ref[...]
    embed_ref[...] = (grad_mixed + mm_nt(grad_mixed.astype(BF16), encw_ref[...])).astype(BF16)


def outer_kernel(n_sec, where, rows_ref, *refs):
    *gots, keep_ref, give_ref, total = refs
    me, odd = where[0], where[1]
    part = rows_ref.shape[1]
    half = keep_ref.shape[0] - EXTRA
    own = 2 * half
    raw = jnp.concatenate([rows_ref[lax.rem(me + n_sec - k, n_sec)] for k in range(n_sec)], axis=0)
    low = jnp.concatenate([g[pl.ds(EXTRA, part), :] for g in gots], axis=0)
    total[...] = mm_tn(raw, low)

    def rows_of(core):
        return total[pl.ds(pl.multiple_of(me * own + core * half, 8), half), :].astype(BF16)

    keep_ref[pl.ds(EXTRA, half), :] = rows_of(odd)
    give_ref[pl.ds(EXTRA, half), :] = rows_of(1 - odd)
    rows = [joined(g) for g in gots]
    gain_row = jnp.zeros_like(rows[0])
    for s in range(n_sec):
        for k in range(n_sec):
            here = lax.rem(me + n_sec - k, n_sec) == s
            gain_row = gain_row + jnp.where(here, rows[k], 0.0)
    extra = split_rows(gain_row)
    keep_ref[pl.ds(0, EXTRA), :] = extra
    give_ref[pl.ds(0, EXTRA), :] = extra


def merge_kernel(*refs):
    *ins, out_ref = refs
    half = out_ref.shape[0] - EXTRA
    gains = [joined(r) for r in ins]
    weights = [r[pl.ds(EXTRA, half), :].astype(F32) for r in ins]
    while len(gains) > 1:
        gains = [a + b for a, b in zip(gains[::2], gains[1::2])]
        weights = [a + b for a, b in zip(weights[::2], weights[1::2])]
    out_ref[pl.ds(0, EXTRA), :] = split_rows(gains[0])
    out_ref[pl.ds(EXTRA, half), :] = weights[0].astype(BF16)


def merged(*parts, **order):
    return call(merge_kernel, [(parts[0].shape, BF16)], *parts, **order)


def spread_kernel(where, own_ref, inc_ref, weight_ref, gain_ref):
    half = own_ref.shape[0] - EXTRA
    odd = where[1]
    for ref, at in ((own_ref, odd), (inc_ref, 1 - odd)):
        weight_ref[pl.ds(pl.multiple_of(at * half, 8), half), :] = ref[pl.ds(EXTRA, half), :].astype(F32)
    gain_ref[...] = joined(own_ref)[0]


def sum_kernel(ats, cut, where, *refs):
    n = len(ats)
    terms, (out_ref, held, total, in_sems, out_sems) = refs[:n], refs[n:]
    rows = out_ref.shape[0]
    size = rows // cut

    def fetch(k, c):
        base = 0 if ats[k] is None else pl.multiple_of(where[ats[k]] * rows, rows)
        source = terms[k].at[pl.ds(base + c * size, size), :]
        return pltpu.make_async_copy(source, held.at[k, pl.ds(c * size, size), :], in_sems.at[k, c])

    def store(c):
        span = pl.ds(c * size, size)
        return pltpu.make_async_copy(total.at[span, :], out_ref.at[span, :], out_sems.at[c])

    for c in range(cut):
        for k in range(n):
            fetch(k, c).start()
    for c in range(cut):
        for k in range(n):
            fetch(k, c).wait()
        span = pl.ds(c * size, size)
        value = held[0, span, :].astype(F32)
        for k in range(1, n):
            value = value + held[k, span, :].astype(F32)
        total[span, :] = value.astype(total.dtype)
        store(c).start()
    for c in range(cut):
        store(c).wait()


def block_sum(rows, dtype, where, *terms):
    cut = 4 if rows % 64 == 0 else 1
    n = len(terms)
    anywhere = pl.BlockSpec(memory_space=pl.ANY)
    return pl.pallas_call(
        functools.partial(sum_kernel, [at for _, at in terms], cut),
        in_specs=[pl.BlockSpec(memory_space=pltpu.SMEM)] + [anywhere] * n,
        out_specs=anywhere,
        out_shape=jax.ShapeDtypeStruct((rows, ENC_D), dtype),
        scratch_shapes=[
            pltpu.VMEM((n, rows, ENC_D), BF16),
            pltpu.VMEM((rows, ENC_D), dtype),
            pltpu.SemaphoreType.DMA((n, cut)),
            pltpu.SemaphoreType.DMA((cut,)),
        ],
        compiler_params=pltpu.CompilerParams(vmem_limit_bytes=LIMIT),
        cost_estimate=SHORT,
    )(where, *[x for x, _ in terms])


def tie(x, *after):
    return lax.optimization_barrier((x, *after))[0]


def rotated(x, n, k):
    return lax.ppermute(x, "section", [(i, (i + k) % n) for i in range(n)]) if k else x


def chunk_at(chips, chip, step, core):
    place = jnp.where(core == 0, chip, chips - 1 - chip)
    ahead = jnp.minimum(chips - step + place, chips - 1)
    return jnp.where(core == 0, ahead, chips - 1 - ahead)


def body(n_sec, n_dp, nbr_embed, enc_weight, enc_gain, kv_weight, queries, pos_bias, nbr_ids, ctx_grad):
    local_rows = nbr_embed[0].reshape(-1, ENC_D)
    part = local_rows.shape[0]
    own = ENC_D // n_sec
    half = own // 2
    chips = n_dp // 2
    kv_rows = 2 * HEADS * HEAD // n_dp
    me = lax.axis_index("section")
    rank = lax.axis_index("dp")
    chip, core = rank // 2, lax.rem(rank, 2)
    near = [(i, i ^ 1) for i in range(n_dp)]

    where = [me, core]
    for step in range(1, chips):
        given = chunk_at(chips, chip, step, 1 - core)
        at = lax.rem(given, chips // 2) * 2 * kv_rows
        where += [at // (STEP * HEAD), given // (chips // 2), lax.rem(at, STEP * HEAD)]
    places = {}
    for step in range(1, chips):
        for j in range(2):
            lane = jnp.where(j == 0, 1 - core, core)
            places[step, j] = len(where), len(where) + 1
            where += [2 * chunk_at(chips, chip, step, core) + lane, 2 * max(step - 2, 0) + lane]
    places["last"] = len(where)
    places["own"] = len(where) + 1
    where += [rank + 1 - 2 * core, rank]
    where = jnp.stack(where).astype(jnp.int32)

    rows = lax.all_gather(local_rows, "section", axis=0, tiled=False)
    grad_query, kv_part, normed, inverse, *rest = layer(
        n_sec, chips - 1, nbr_ids[0], where, rows, enc_weight, enc_gain, kv_weight[0], queries[0], pos_bias[0], ctx_grad[0]
    )
    kv_part = kv_part.reshape(-1, ENC_D)
    grad_enc, gives = rest[:n_sec], rest[n_sec:]

    got = [rotated(grad_enc[k], n_sec, k) for k in range(n_sec)]
    incoming = [None, None]
    state = {"kv": kv_part, "sums": []}

    def kv_step(step):
        hops = [(2 * a, 2 * a + 2) for a in range(step)]
        hops += [(2 * (chips - 1 - a) + 1, 2 * (chips - 2 - a) + 1) for a in range(step)]
        for j in range(2):
            block, lane = places[step, j]
            terms = [(tie(state["kv"], *state["sums"]), block), (paired[min(step, 2) - 1], lane)]
            if incoming[j] is not None:
                terms.append((incoming[j], None))
            out = block_sum(kv_rows, BF16, where, *terms)
            incoming[j] = lax.ppermute(out, "dp", hops)
            state["sums"].append(out)

    def last_pair():
        out = block_sum(kv_rows, BF16, where, (state["kv"], places["last"]), (incoming[0], None))
        state["swapped"] = lax.ppermute(out, "dp", near)
        state["sums"].append(out)

    def order():
        sums, state["sums"] = state["sums"], []
        return {"after": sums, "carry": [state["kv"]]}

    def finish_stage():
        held = order()
        held["after"] = held["after"] + paired[1:]
        state["mixed"], send, state["kv"] = call(
            finish_kernel,
            [((part, ENC_D), F32), ((EXTRA + part, ENC_D), BF16)],
            *got, normed, inverse, enc_gain, **held,
        )
        state["lows"] = [rotated(send, n_sec, k) for k in range(n_sec)]

    def outer_stage():
        shape = ((EXTRA + half, ENC_D), BF16)
        *state["halves"], state["kv"] = call(
            functools.partial(outer_kernel, n_sec),
            [shape, shape],
            where, rows, *state["lows"],
            scalars=1,
            scratch_shapes=[pltpu.VMEM((ENC_D, ENC_D), F32)],
            **order(),
        )

    def swap(x, dist):
        return lax.ppermute(x, "dp", [(i, i ^ dist) for i in range(n_dp)])

    def quad_stage():
        keep, give = state["halves"]
        parts = [keep, swap(give, 1)] + ([swap(keep, 2), swap(give, 3)] if chips > 1 else [])
        state["payload"], state["kv"] = merged(*parts, **order())

    def embed_stage():
        (state["embed"],) = call(embed_kernel, [((part, ENC_D), BF16)], state["mixed"], enc_weight, after=[state["payload"]])

    def merge_stage(dist):
        payload = state["payload"]
        state["payload"], state["kv"] = merged(payload, swap(payload, dist), **order())

    paired = [lax.ppermute(g, "dp", near) for g in gives]
    merges = [functools.partial(merge_stage, 2 << k) for k in range(1, (chips - 1).bit_length())]
    enc_chain = [finish_stage, outer_stage, quad_stage] + merges
    kv_chain = [functools.partial(kv_step, step) for step in range(1, chips)] + [last_pair]
    for at in range(max(len(kv_chain), len(enc_chain))):
        for chain in (kv_chain, enc_chain):
            if at < len(chain):
                chain[at]()
        if at == 2:
            embed_stage()
    payload = state["payload"]
    other = lax.ppermute(payload, "dp", near)
    weight_grad, gain_row, kv_own = call(
        spread_kernel, [((own, ENC_D), F32), ((ENC_D,), F32)], where, payload, other, scalars=1, **order(),
    )
    kv_grad = block_sum(kv_rows, F32, where, (kv_own, places["own"]), (state["swapped"], None), (incoming[1], None))
    embed_grad = state["embed"]
    return (
        grad_query[None],
        kv_grad[None],
        weight_grad,
        gain_row,
        embed_grad.reshape(nbr_embed.shape),
    )


def solution(mesh):
    return jax.shard_map(
        functools.partial(body, mesh.shape["section"], mesh.shape["dp"]),
        mesh=mesh,
        in_specs=(
            P("dp", None, "section", None),
            P(),
            P(),
            P("section", None, None),
            P("section", "dp", None),
            P("section", None, None, None),
            P("dp", None, None),
            P("section", "dp", None),
        ),
        out_specs=(
            P("section", "dp", None),
            P("section", "dp", None),
            P("section", None),
            P(),
            P("dp", None, "section", None),
        ),
        check_vma=False,
    )
```

```python
import functools
import math

import jax
import jax.numpy as jnp
from jax import lax
from jax.experimental import pallas as pl
from jax.experimental.pallas import tpu as pltpu
from jax.sharding import PartitionSpec as P

HEADS = 16
HEAD = 128
ENC_D = 896
BLOCK = 64
NBR = 2
NLEN = 128
TOK_DEV = 128
NSET = 4
PAIR = 2
STEP = 4
EXTRA = 16

eps_norm = 1e-06
LIMIT = 65400 * 1024
SHORT = pl.CostEstimate(flops=1, bytes_accessed=1, transcendentals=0)
LONGER = pl.CostEstimate(flops=20_000_000_000, bytes_accessed=1_000_000, transcendentals=0)
F32 = jnp.float32
BF16 = jnp.bfloat16


def mm(a, b):
    return lax.dot_general(a, b, (((1,), (0,)), ((), ())), preferred_element_type=F32)


def mm_nt(a, b):
    return lax.dot_general(a, b, (((1,), (1,)), ((), ())), preferred_element_type=F32)


def mm_tn(a, b):
    return lax.dot_general(a, b, (((0,), (0,)), ((), ())), preferred_element_type=F32)


def chunk_order(chips, width):
    rows = 2 * HEADS * HEAD // chips
    return max(1, rows // width), max(1, width // rows)


def normalised(raw, encw_ref):
    mixed = raw.astype(F32) + mm(raw, encw_ref[...])
    inverse = lax.rsqrt(jnp.mean(mixed * mixed, axis=-1, keepdims=True) + eps_norm)
    return mixed * inverse, inverse


def layer_kernel(
    n_sec, chips, ids, where, *refs,
):
    rows_refs, (encw_ref, gain_ref, w_ref, q_ref, bias_ref, up_ref) = refs[:n_sec], refs[n_sec:n_sec + 6]
    qg_ref, first_ref, second_ref, normed_ref, inverse_ref, *rest = refs[n_sec + 6:]
    ge_refs, (enc, proj, total, gset, acc) = rest[:n_sec], rest[n_sec:]
    step = pl.program_id(0)
    part = NLEN // n_sec
    blocks = TOK_DEV // BLOCK
    width = STEP * HEAD
    factor = 1.0 / math.sqrt(HEAD)

    @pl.when(step == 0)
    def _():
        for k in range(n_sec):
            s = lax.rem(where[0] + n_sec - k, n_sec)
            for e in range(NSET):
                span = pl.ds(pl.multiple_of(e * NLEN + s * part, part), part)
                enc[span, :] = rows_refs[k][pl.ds(e * part, part), :]
        normed, _ = normalised(enc[...], encw_ref)
        enc[...] = (normed * gain_ref[...][None, :]).astype(BF16)
        normed, inverse = normalised(rows_refs[0][...], encw_ref)
        normed_ref[...] = normed
        inverse_ref[...] = jnp.broadcast_to(inverse, inverse_ref.shape)
        acc[...] = jnp.zeros_like(acc)

    encoded = enc[...]
    weights = w_ref[...].reshape(2 * width, ENC_D)
    proj[...] = mm_nt(encoded, weights).astype(BF16)
    total[...] = jnp.zeros_like(total)
    spans = [
        [pl.ds(pl.multiple_of(ids[c, n] * NLEN, NLEN), NLEN) for n in range(NBR)]
        for c in range(blocks)
    ]
    toks = [slice(c * BLOCK, (c + 1) * BLOCK) for c in range(blocks)]
    pair = PAIR * HEAD
    items = [(c, g) for c in range(blocks) for g in range(STEP // PAIR)]

    def stacked(ref, c, g):
        x = ref[toks[c], g * pair:(g + 1) * pair]
        head_of = lax.broadcasted_iota(jnp.int32, x.shape, 1) // HEAD
        return jnp.concatenate([jnp.where(head_of == h, x, jnp.zeros_like(x)) for h in range(PAIR)], axis=0)

    def picked(c, g, base):
        return jnp.concatenate([proj[s, base + g * pair:base + (g + 1) * pair] for s in spans[c]], axis=0)

    def bias(g):
        return jnp.concatenate([bias_ref[g * PAIR + h] for h in range(PAIR)], axis=0).astype(F32)

    keys = {i: picked(*i, 0) for i in items}
    values = {i: picked(*i, width) for i in items}
    query = {i: stacked(q_ref, *i) for i in items}
    upstream = {i: stacked(up_ref, *i) for i in items}
    scores = {i: mm_nt(query[i], keys[i]) * factor + bias(i[1]) for i in items}
    dprobs = {i: mm_nt(upstream[i], values[i]) for i in items}
    exps = {i: jnp.exp(scores[i] - jnp.max(scores[i], axis=-1, keepdims=True)) for i in items}
    probs = {i: exps[i] / jnp.sum(exps[i], axis=-1, keepdims=True) for i in items}
    dvalues = {i: mm_tn(probs[i].astype(BF16), upstream[i]) for i in items}
    inner = {i: jnp.sum(probs[i] * dprobs[i], axis=-1, keepdims=True) for i in items}
    dscores = {i: (probs[i] * (dprobs[i] - inner[i])).astype(BF16) for i in items}
    dkeys = {i: mm_tn(dscores[i], query[i]) * factor for i in items}
    dquery = {i: mm(dscores[i], keys[i]) * factor for i in items}
    for c, g in items:
        for h in range(PAIR):
            col = slice(h * HEAD, (h + 1) * HEAD)
            qg_ref[toks[c], g * pair + h * HEAD:g * pair + (h + 1) * HEAD] = (
                dquery[c, g][h * BLOCK:(h + 1) * BLOCK, col].astype(BF16)
            )
        for n, s in enumerate(spans[c]):
            total[s, g * pair:(g + 1) * pair] += dkeys[c, g][n * NLEN:(n + 1) * NLEN]
            total[s, width + g * pair:width + (g + 1) * pair] += dvalues[c, g][n * NLEN:(n + 1) * NLEN]
    gset[...] = total[...].astype(BF16)
    acc[...] += mm(gset[...], weights)
    kv = mm_tn(gset[...], encoded).astype(BF16)
    keys_part, values_part = kv[:width], kv[width:]
    _, inside = chunk_order(chips, width)
    size = width // inside
    values_part = jnp.concatenate([values_part[u * size:(u + 1) * size] for u in reversed(range(inside))], axis=0)
    low = where[1] == 0
    first_ref[...] = jnp.where(low, keys_part, values_part)
    second_ref[...] = jnp.where(low, values_part, keys_part)

    @pl.when(step == pl.num_programs(0) - 1)
    def _():
        for k in range(n_sec):
            s = lax.rem(where[0] + k, n_sec)
            for e in range(NSET):
                span = pl.ds(pl.multiple_of(e * NLEN + s * part, part), part)
                ge_refs[k][pl.ds(e * part, part), :] = acc[span, :].astype(BF16)


def layer(n_sec, chips, ids, where, rows, enc_weight, gain, weights, queries, bias, upstream):
    head_width = HEADS * HEAD
    width = STEP * HEAD
    steps = HEADS // STEP
    all_rows = NSET * NLEN
    part = all_rows // n_sec
    blocks, _ = chunk_order(chips, width)

    def half(core):
        def at(i, ids, where):
            turned = (steps // blocks - 1 - i // blocks) * blocks + lax.rem(i, blocks)
            return jnp.where(where[1] == core, i, turned), 0

        return pl.BlockSpec((width, ENC_D), at)

    fixed2 = lambda i, *_: (0, 0)
    fixed3 = lambda i, *_: (0, 0, 0)
    return pl.pallas_call(
        functools.partial(layer_kernel, n_sec, chips),
        grid_spec=pltpu.PrefetchScalarGridSpec(
            num_scalar_prefetch=2,
            grid=(steps,),
            in_specs=[
                *[pl.BlockSpec((part, ENC_D), fixed2)] * n_sec,
                pl.BlockSpec((ENC_D, ENC_D), fixed2),
                pl.BlockSpec((ENC_D,), lambda i, *_: (0,)),
                pl.BlockSpec((2, width, ENC_D), lambda i, *_: (0, i, 0)),
                pl.BlockSpec((TOK_DEV, width), lambda i, *_: (0, i)),
                pl.BlockSpec((STEP, BLOCK, NBR * NLEN), lambda i, *_: (i, 0, 0)),
                pl.BlockSpec((TOK_DEV, width), lambda i, *_: (0, i)),
            ],
            out_specs=[
                pl.BlockSpec((TOK_DEV, width), lambda i, *_: (0, i)),
                half(0),
                half(1),
                pl.BlockSpec((part, ENC_D), fixed2),
                pl.BlockSpec((part, HEAD), fixed2),
            ]
            + [pl.BlockSpec((part, ENC_D), fixed2)] * n_sec,
            scratch_shapes=[
                pltpu.VMEM((all_rows, ENC_D), BF16),
                pltpu.VMEM((all_rows, 2 * width), BF16),
                pltpu.VMEM((all_rows, 2 * width), F32),
                pltpu.VMEM((all_rows, 2 * width), BF16),
                pltpu.VMEM((all_rows, ENC_D), F32),
            ],
        ),
        out_shape=[
            jax.ShapeDtypeStruct((TOK_DEV, head_width), BF16),
            jax.ShapeDtypeStruct((head_width, ENC_D), BF16),
            jax.ShapeDtypeStruct((head_width, ENC_D), BF16),
            jax.ShapeDtypeStruct((part, ENC_D), F32),
            jax.ShapeDtypeStruct((part, HEAD), F32),
        ]
        + [jax.ShapeDtypeStruct((part, ENC_D), BF16)] * n_sec,
        compiler_params=pltpu.CompilerParams(
            vmem_limit_bytes=LIMIT, dimension_semantics=("arbitrary",)
        ),
        cost_estimate=SHORT,
    )(ids, where, *rows, enc_weight, gain, weights.reshape(2, head_width, ENC_D), queries, bias, upstream)


def call(kernel, outs, *args, after=(), carry=(), scalars=0, scratch_shapes=()):
    n_in, n_out, n_extra, n_carry = len(args), len(outs), len(after), len(carry)

    def inner(*refs):
        own = refs[n_in + n_extra + n_carry:]
        kernel(*refs[:n_in], *own[:n_out], *own[n_out + n_carry:])

    vmem, anywhere = pl.BlockSpec(memory_space=pltpu.VMEM), pl.BlockSpec(memory_space=pl.ANY)
    return pl.pallas_call(
        inner,
        in_specs=[pl.BlockSpec(memory_space=pltpu.SMEM)] * scalars
        + [vmem] * (n_in - scalars)
        + [anywhere] * (n_extra + n_carry),
        out_specs=[vmem] * n_out + [anywhere] * n_carry,
        out_shape=[jax.ShapeDtypeStruct(shape, dtype) for shape, dtype in outs]
        + [jax.ShapeDtypeStruct(x.shape, x.dtype) for x in carry],
        input_output_aliases={n_in + n_extra + k: n_out + k for k in range(n_carry)},
        scratch_shapes=scratch_shapes,
        compiler_params=pltpu.CompilerParams(vmem_limit_bytes=LIMIT),
        cost_estimate=LONGER,
    )(*args, *after, *carry)


def split_rows(row):
    high = row.astype(BF16).astype(F32)
    at = lax.broadcasted_iota(jnp.int32, (EXTRA, row.shape[-1]), 0)
    return jnp.where(at == 0, high, jnp.where(at == 1, row - high, 0.0)).astype(BF16)


def joined(ref):
    extra = ref[pl.ds(0, EXTRA), :].astype(F32)
    return extra[0:1] + extra[1:2]


def finish_kernel(*refs):
    *grads, normed_ref, inverse_ref, gain_ref, mixed_ref, send_ref = refs
    grad = grads[0][...].astype(F32)
    for g in grads[1:]:
        grad = grad + g[...].astype(F32)
    normed = normed_ref[...]
    grad_normed = grad * gain_ref[...][None, :]
    grad_mixed = inverse_ref[...][:, :1] * (
        grad_normed - normed * jnp.mean(grad_normed * normed, axis=-1, keepdims=True)
    )
    mixed_ref[...] = grad_mixed
    send_ref[pl.ds(0, EXTRA), :] = split_rows(jnp.sum(grad * normed, axis=0, keepdims=True))
    send_ref[pl.ds(EXTRA, normed.shape[0]), :] = grad_mixed.astype(BF16)


def embed_kernel(mixed_ref, encw_ref, embed_ref):
    grad_mixed = mixed_ref[...]
    embed_ref[...] = (grad_mixed + mm_nt(grad_mixed.astype(BF16), encw_ref[...])).astype(BF16)


def outer_kernel(n_sec, where, *refs):
    rows_refs, gots, (keep_ref, give_ref, total) = refs[:n_sec], refs[n_sec:2 * n_sec], refs[2 * n_sec:]
    me, odd = where[0], where[1]
    part = rows_refs[0].shape[0]
    half = keep_ref.shape[0] - EXTRA
    own = 2 * half
    raw = jnp.concatenate([r[...] for r in rows_refs], axis=0)
    low = jnp.concatenate([g[pl.ds(EXTRA, part), :] for g in gots], axis=0)
    total[...] = mm_tn(raw, low)

    def rows_of(core):
        return total[pl.ds(pl.multiple_of(me * own + core * half, 8), half), :].astype(BF16)

    keep_ref[pl.ds(EXTRA, half), :] = rows_of(odd)
    give_ref[pl.ds(EXTRA, half), :] = rows_of(1 - odd)
    rows = [joined(g) for g in gots]
    gain_row = jnp.zeros_like(rows[0])
    for s in range(n_sec):
        for k in range(n_sec):
            here = lax.rem(me + n_sec - k, n_sec) == s
            gain_row = gain_row + jnp.where(here, rows[k], 0.0)
    extra = split_rows(gain_row)
    keep_ref[pl.ds(0, EXTRA), :] = extra
    give_ref[pl.ds(0, EXTRA), :] = extra


def merge_kernel(*refs):
    *ins, out_ref = refs
    half = out_ref.shape[0] - EXTRA
    gains = [joined(r) for r in ins]
    weights = [r[pl.ds(EXTRA, half), :].astype(F32) for r in ins]
    while len(gains) > 1:
        gains = [a + b for a, b in zip(gains[::2], gains[1::2])]
        weights = [a + b for a, b in zip(weights[::2], weights[1::2])]
    out_ref[pl.ds(0, EXTRA), :] = split_rows(gains[0])
    out_ref[pl.ds(EXTRA, half), :] = weights[0].astype(BF16)


def merged(*parts, **order):
    return call(merge_kernel, [(parts[0].shape, BF16)], *parts, **order)


def spread_kernel(where, own_ref, inc_ref, weight_ref, gain_ref):
    half = own_ref.shape[0] - EXTRA
    odd = where[1]
    for ref, at in ((own_ref, odd), (inc_ref, 1 - odd)):
        weight_ref[pl.ds(pl.multiple_of(at * half, 8), half), :] = ref[pl.ds(EXTRA, half), :].astype(F32)
    gain_ref[...] = joined(own_ref)[0]


def sum_kernel(plan, cut, where, *refs):
    n = len(plan)
    count = sum(arrays for arrays, _, _ in plan)
    sources, (out_ref, held, total, in_sems, out_sems) = refs[:count], refs[count:]
    rows = out_ref.shape[0]
    size = rows // cut

    def fetch(k, c, which=0):
        start = sum(arrays for arrays, _, _ in plan[:k])
        block = plan[k][1]
        base = 0 if block is None else pl.multiple_of(where[block] * rows, rows)
        source = sources[start + which].at[pl.ds(base + c * size, size), :]
        return pltpu.make_async_copy(source, held.at[k, pl.ds(c * size, size), :], in_sems.at[k, c])

    def store(c):
        span = pl.ds(c * size, size)
        return pltpu.make_async_copy(total.at[span, :], out_ref.at[span, :], out_sems.at[c])

    for c in range(cut):
        for k, (arrays, _, choice) in enumerate(plan):
            if arrays == 1:
                fetch(k, c).start()
                continue
            for which in range(arrays):
                pl.when(where[choice] == which)(fetch(k, c, which).start)
    for c in range(cut):
        for k in range(n):
            fetch(k, c).wait()
        span = pl.ds(c * size, size)
        value = held[0, span, :].astype(F32)
        for k in range(1, n):
            value = value + held[k, span, :].astype(F32)
        total[span, :] = value.astype(total.dtype)
        store(c).start()
    for c in range(cut):
        store(c).wait()


def block_sum(rows, dtype, where, *terms):
    cut = 2 if rows % 32 == 0 else 1
    n = len(terms)
    sources = [x for arrays, _, _ in terms for x in arrays]
    anywhere = pl.BlockSpec(memory_space=pl.ANY)
    return pl.pallas_call(
        functools.partial(sum_kernel, [(len(arrays), block, choice) for arrays, block, choice in terms], cut),
        in_specs=[pl.BlockSpec(memory_space=pltpu.SMEM)] + [anywhere] * len(sources),
        out_specs=anywhere,
        out_shape=jax.ShapeDtypeStruct((rows, ENC_D), dtype),
        scratch_shapes=[
            pltpu.VMEM((n, rows, ENC_D), BF16),
            pltpu.VMEM((rows, ENC_D), dtype),
            pltpu.SemaphoreType.DMA((n, cut)),
            pltpu.SemaphoreType.DMA((cut,)),
        ],
        compiler_params=pltpu.CompilerParams(vmem_limit_bytes=LIMIT),
        cost_estimate=SHORT,
    )(where, *sources)


def rotated(x, n, k):
    return lax.ppermute(x, "section", [(i, (i + k) % n) for i in range(n)]) if k else x


def chunk_at(chips, chip, step, core):
    place = jnp.where(core == 0, chip, chips - 1 - chip)
    ahead = jnp.minimum(chips - step + place, chips - 1)
    return jnp.where(core == 0, ahead, chips - 1 - ahead)


def body(n_sec, n_dp, nbr_embed, enc_weight, enc_gain, kv_weight, queries, pos_bias, nbr_ids, ctx_grad):
    local_rows = nbr_embed[0].reshape(-1, ENC_D)
    part = local_rows.shape[0]
    own = ENC_D // n_sec
    half = own // 2
    chips = n_dp // 2
    kv_rows = 2 * HEADS * HEAD // n_dp
    me = lax.axis_index("section")
    rank = lax.axis_index("dp")
    chip, core = rank // 2, lax.rem(rank, 2)
    near = [(i, i ^ 1) for i in range(n_dp)]

    early = chips // 2
    where, places = [me, core], {}

    def place(name, chunk, lane):
        keyed = chunk < chips // 2
        spot = jnp.where(keyed, chunk, chips - 1 - chunk)
        mine = jnp.where(keyed, core, 1 - core)
        places[name] = range(len(where), len(where) + 3)
        where.extend([2 * spot + lane, mine, 1 - mine])

    for step in range(1, chips):
        for j, lane in enumerate((1 - core, core)):
            place((step, j), chunk_at(chips, chip, step, core), lane)
    place("other", chip, 1 - core)
    place("own", chip, core)
    where = jnp.stack(where).astype(jnp.int32)
    spot = where[:2]

    rows = [rotated(local_rows, n_sec, k) for k in range(n_sec)]
    grad_query, first, second, normed, inverse, *grad_enc = layer(
        n_sec, chips, nbr_ids[0], where, rows, enc_weight, enc_gain, kv_weight[0], queries[0], pos_bias[0], ctx_grad[0]
    )
    got = [rotated(grad_enc[k], n_sec, k) for k in range(n_sec)]
    incoming = [None, None]
    state = {"where": where, "sums": []}
    mine = [first, second]
    theirs = [lax.ppermute(x, "dp", near) for x in mine]

    def kv_step(step):
        hops = [(2 * a, 2 * a + 2) for a in range(step)]
        hops += [(2 * (chips - 1 - a) + 1, 2 * (chips - 2 - a) + 1) for a in range(step)]
        for j in range(2):
            block, here, there = places[step, j]
            if step <= early:
                terms = [(mine[1:], block, None), (theirs[:1], block, None)]
            else:
                terms = [(mine, block, here), (theirs, block, there)]
            if incoming[j] is not None:
                terms.append(([incoming[j]], None, None))
            out = block_sum(kv_rows, BF16, state["where"], *terms)
            incoming[j] = lax.ppermute(out, "dp", hops)
            state["sums"].append(out)

    def last_pair():
        block, here, _ = places["other"]
        out = block_sum(kv_rows, BF16, state["where"], (mine, block, here), ([incoming[0]], None, None))
        state["swapped"] = lax.ppermute(out, "dp", near)
        state["sums"].append(out)

    def order():
        sums, state["sums"] = state["sums"], []
        return {"after": sums, "carry": [state["where"]]}

    def finish_stage():
        held = order()
        held["after"] = held["after"] + theirs[1:]
        state["mixed"], send, state["where"] = call(
            finish_kernel,
            [((part, ENC_D), F32), ((EXTRA + part, ENC_D), BF16)],
            *got, normed, inverse, enc_gain, **held,
        )
        state["lows"] = [rotated(send, n_sec, k) for k in range(n_sec)]

    def outer_stage():
        shape = ((EXTRA + half, ENC_D), BF16)
        *state["halves"], state["where"] = call(
            functools.partial(outer_kernel, n_sec),
            [shape, shape],
            spot, *rows, *state["lows"],
            scalars=1,
            scratch_shapes=[pltpu.VMEM((ENC_D, ENC_D), F32)],
            **order(),
        )

    def swap(x, dist):
        return lax.ppermute(x, "dp", [(i, i ^ dist) for i in range(n_dp)])

    def quad_stage():
        keep, give = state["halves"]
        parts = [keep, swap(give, 1)] + ([swap(keep, 2), swap(give, 3)] if chips > 1 else [])
        state["payload"], state["where"] = merged(*parts, **order())

    def embed_stage():
        (state["embed"],) = call(embed_kernel, [((part, ENC_D), BF16)], state["mixed"], enc_weight, after=[state["payload"]])

    def merge_stage(dist):
        payload = state["payload"]
        state["payload"], state["where"] = merged(payload, swap(payload, dist), **order())

    merges = [functools.partial(merge_stage, 2 << k) for k in range(1, (chips - 1).bit_length())]
    enc_chain = [finish_stage, outer_stage, quad_stage] + merges
    kv_chain = [functools.partial(kv_step, step) for step in range(1, chips)] + [last_pair]
    for at in range(max(len(kv_chain), len(enc_chain))):
        for chain in (kv_chain, enc_chain):
            if at < len(chain):
                chain[at]()
        if at == 2:
            embed_stage()
    payload = state["payload"]
    other = lax.ppermute(payload, "dp", near)
    weight_grad, gain_row, table = call(
        spread_kernel, [((own, ENC_D), F32), ((ENC_D,), F32)], spot, payload, other,
        scalars=1, **order(),
    )
    block, here, _ = places["own"]
    kv_grad = block_sum(
        kv_rows, F32, table, (mine, block, here), ([state["swapped"]], None, None), ([incoming[1]], None, None)
    )
    embed_grad = state["embed"]
    return (
        grad_query[None],
        kv_grad[None],
        weight_grad,
        gain_row,
        embed_grad.reshape(nbr_embed.shape),
    )


def solution(mesh):
    return jax.shard_map(
        functools.partial(body, mesh.shape["section"], mesh.shape["dp"]),
        mesh=mesh,
        in_specs=(
            P("dp", None, "section", None),
            P(),
            P(),
            P("section", None, None),
            P("section", "dp", None),
            P("section", None, None, None),
            P("dp", None, None),
            P("section", "dp", None),
        ),
        out_specs=(
            P("section", "dp", None),
            P("section", "dp", None),
            P("section", None),
            P(),
            P("dp", None, "section", None),
        ),
        check_vma=False,
    )
```

```python
import functools
import math

import jax
import jax.numpy as jnp
from jax import lax
from jax.experimental import pallas as pl
from jax.experimental.pallas import tpu as pltpu
from jax.sharding import PartitionSpec as P

HEADS = 16
HEAD = 128
ENC_D = 896
BLOCK = 64
NBR = 2
NLEN = 128
TOK_DEV = 128
NSET = 4
PAIR = 2
STEP = 4
EXTRA = 16

eps_norm = 1e-06
LIMIT = 65400 * 1024
SHORT = pl.CostEstimate(flops=1, bytes_accessed=1, transcendentals=0)
LONGER = pl.CostEstimate(flops=20_000_000_000, bytes_accessed=1_000_000, transcendentals=0)
F32 = jnp.float32
BF16 = jnp.bfloat16


def mm(a, b):
    return lax.dot_general(a, b, (((1,), (0,)), ((), ())), preferred_element_type=F32)


def mm_nt(a, b):
    return lax.dot_general(a, b, (((1,), (1,)), ((), ())), preferred_element_type=F32)


def mm_tn(a, b):
    return lax.dot_general(a, b, (((0,), (0,)), ((), ())), preferred_element_type=F32)


def chunk_order(chips, width):
    rows = 2 * HEADS * HEAD // chips
    return max(1, rows // width), max(1, width // rows)


def normalised(raw, encw_ref):
    mixed = raw.astype(F32) + mm(raw, encw_ref[...])
    inverse = lax.rsqrt(jnp.mean(mixed * mixed, axis=-1, keepdims=True) + eps_norm)
    return mixed * inverse, inverse


def layer_kernel(
    n_sec, chips, ids, where, *refs,
):
    rows_refs, (encw_ref, gain_ref, w_ref, q_ref, bias_ref, up_ref) = refs[:n_sec], refs[n_sec:n_sec + 6]
    qg_ref, first_ref, second_ref, *rest = refs[n_sec + 6:]
    ge_refs, (enc, proj, total, gset, acc) = rest[:n_sec], rest[n_sec:]
    step = pl.program_id(0)
    part = NLEN // n_sec
    blocks = TOK_DEV // BLOCK
    width = STEP * HEAD
    factor = 1.0 / math.sqrt(HEAD)

    @pl.when(step == 0)
    def _():
        def places(k):
            s = lax.rem(where[0] + n_sec - k, n_sec)
            return [(e, pl.ds(pl.multiple_of(e * NLEN + s * part, part), part)) for e in range(NSET)]

        others = jnp.concatenate([r[...] for r in rows_refs[1:]], axis=0)
        normed, _ = normalised(others, encw_ref)
        encoded = (normed * gain_ref[...][None, :]).astype(BF16)
        for e, span in places(0):
            enc[span, :] = rows_refs[0][pl.ds(e * part, part), :]
        for k in range(1, n_sec):
            for e, span in places(k):
                at = ((k - 1) * NSET + e) * part
                enc[span, :] = encoded[at:at + part]
        acc[...] = jnp.zeros_like(acc)

    encoded = enc[...]
    weights = w_ref[...].reshape(2 * width, ENC_D)
    proj[...] = mm_nt(encoded, weights).astype(BF16)
    total[...] = jnp.zeros_like(total)
    spans = [
        [pl.ds(pl.multiple_of(ids[c, n] * NLEN, NLEN), NLEN) for n in range(NBR)]
        for c in range(blocks)
    ]
    toks = [slice(c * BLOCK, (c + 1) * BLOCK) for c in range(blocks)]
    pair = PAIR * HEAD
    items = [(c, g) for c in range(blocks) for g in range(STEP // PAIR)]

    def stacked(ref, c, g):
        x = ref[toks[c], g * pair:(g + 1) * pair]
        head_of = lax.broadcasted_iota(jnp.int32, x.shape, 1) // HEAD
        return jnp.concatenate([jnp.where(head_of == h, x, jnp.zeros_like(x)) for h in range(PAIR)], axis=0)

    def picked(c, g, base):
        return jnp.concatenate([proj[s, base + g * pair:base + (g + 1) * pair] for s in spans[c]], axis=0)

    def bias(g):
        return jnp.concatenate([bias_ref[g * PAIR + h] for h in range(PAIR)], axis=0).astype(F32)

    keys = {i: picked(*i, 0) for i in items}
    values = {i: picked(*i, width) for i in items}
    query = {i: stacked(q_ref, *i) for i in items}
    upstream = {i: stacked(up_ref, *i) for i in items}
    scores = {i: mm_nt(query[i], keys[i]) * factor + bias(i[1]) for i in items}
    dprobs = {i: mm_nt(upstream[i], values[i]) for i in items}
    exps = {i: jnp.exp(scores[i] - jnp.max(scores[i], axis=-1, keepdims=True)) for i in items}
    probs = {i: exps[i] / jnp.sum(exps[i], axis=-1, keepdims=True) for i in items}
    dvalues = {i: mm_tn(probs[i].astype(BF16), upstream[i]) for i in items}
    inner = {i: jnp.sum(probs[i] * dprobs[i], axis=-1, keepdims=True) for i in items}
    dscores = {i: (probs[i] * (dprobs[i] - inner[i])).astype(BF16) for i in items}
    dkeys = {i: mm_tn(dscores[i], query[i]) * factor for i in items}
    dquery = {i: mm(dscores[i], keys[i]) * factor for i in items}
    for c, g in items:
        for h in range(PAIR):
            col = slice(h * HEAD, (h + 1) * HEAD)
            qg_ref[toks[c], g * pair + h * HEAD:g * pair + (h + 1) * HEAD] = (
                dquery[c, g][h * BLOCK:(h + 1) * BLOCK, col].astype(BF16)
            )
        for n, s in enumerate(spans[c]):
            total[s, g * pair:(g + 1) * pair] += dkeys[c, g][n * NLEN:(n + 1) * NLEN]
            total[s, width + g * pair:width + (g + 1) * pair] += dvalues[c, g][n * NLEN:(n + 1) * NLEN]
    gset[...] = total[...].astype(BF16)
    acc[...] += mm(gset[...], weights)
    kv = mm_tn(gset[...], encoded).astype(BF16)
    keys_part, values_part = kv[:width], kv[width:]
    _, inside = chunk_order(chips, width)
    size = width // inside
    values_part = jnp.concatenate([values_part[u * size:(u + 1) * size] for u in reversed(range(inside))], axis=0)
    low = where[1] == 0
    first_ref[...] = jnp.where(low, keys_part, values_part)
    second_ref[...] = jnp.where(low, values_part, keys_part)

    @pl.when(step == pl.num_programs(0) - 1)
    def _():
        for k in range(n_sec):
            s = lax.rem(where[0] + k, n_sec)
            for e in range(NSET):
                span = pl.ds(pl.multiple_of(e * NLEN + s * part, part), part)
                ge_refs[k][pl.ds(e * part, part), :] = acc[span, :].astype(BF16)


def layer(n_sec, chips, ids, where, rows, enc_weight, gain, weights, queries, bias, upstream):
    head_width = HEADS * HEAD
    width = STEP * HEAD
    steps = HEADS // STEP
    all_rows = NSET * NLEN
    part = all_rows // n_sec
    blocks, _ = chunk_order(chips, width)

    def half(core):
        def at(i, ids, where):
            turned = (steps // blocks - 1 - i // blocks) * blocks + lax.rem(i, blocks)
            return jnp.where(where[1] == core, i, turned), 0

        return pl.BlockSpec((width, ENC_D), at)

    fixed2 = lambda i, *_: (0, 0)
    fixed3 = lambda i, *_: (0, 0, 0)
    return pl.pallas_call(
        functools.partial(layer_kernel, n_sec, chips),
        grid_spec=pltpu.PrefetchScalarGridSpec(
            num_scalar_prefetch=2,
            grid=(steps,),
            in_specs=[
                *[pl.BlockSpec((part, ENC_D), fixed2)] * n_sec,
                pl.BlockSpec((ENC_D, ENC_D), fixed2),
                pl.BlockSpec((ENC_D,), lambda i, *_: (0,)),
                pl.BlockSpec((2, width, ENC_D), lambda i, *_: (0, i, 0)),
                pl.BlockSpec((TOK_DEV, width), lambda i, *_: (0, i)),
                pl.BlockSpec((STEP, BLOCK, NBR * NLEN), lambda i, *_: (i, 0, 0)),
                pl.BlockSpec((TOK_DEV, width), lambda i, *_: (0, i)),
            ],
            out_specs=[
                pl.BlockSpec((TOK_DEV, width), lambda i, *_: (0, i)),
                half(0),
                half(1),
            ]
            + [pl.BlockSpec((part, ENC_D), fixed2)] * n_sec,
            scratch_shapes=[
                pltpu.VMEM((all_rows, ENC_D), BF16),
                pltpu.VMEM((all_rows, 2 * width), BF16),
                pltpu.VMEM((all_rows, 2 * width), F32),
                pltpu.VMEM((all_rows, 2 * width), BF16),
                pltpu.VMEM((all_rows, ENC_D), F32),
            ],
        ),
        out_shape=[
            jax.ShapeDtypeStruct((TOK_DEV, head_width), BF16),
            jax.ShapeDtypeStruct((head_width, ENC_D), BF16),
            jax.ShapeDtypeStruct((head_width, ENC_D), BF16),
        ]
        + [jax.ShapeDtypeStruct((part, ENC_D), BF16)] * n_sec,
        compiler_params=pltpu.CompilerParams(
            vmem_limit_bytes=LIMIT, dimension_semantics=("arbitrary",)
        ),
        cost_estimate=SHORT,
    )(ids, where, *rows, enc_weight, gain, weights.reshape(2, head_width, ENC_D), queries, bias, upstream)


def call(kernel, outs, *args, after=(), carry=(), scalars=0, scratch_shapes=()):
    n_in, n_out, n_extra, n_carry = len(args), len(outs), len(after), len(carry)

    def inner(*refs):
        own = refs[n_in + n_extra + n_carry:]
        kernel(*refs[:n_in], *own[:n_out], *own[n_out + n_carry:])

    vmem, anywhere = pl.BlockSpec(memory_space=pltpu.VMEM), pl.BlockSpec(memory_space=pl.ANY)
    return pl.pallas_call(
        inner,
        in_specs=[pl.BlockSpec(memory_space=pltpu.SMEM)] * scalars
        + [vmem] * (n_in - scalars)
        + [anywhere] * (n_extra + n_carry),
        out_specs=[vmem] * n_out + [anywhere] * n_carry,
        out_shape=[jax.ShapeDtypeStruct(shape, dtype) for shape, dtype in outs]
        + [jax.ShapeDtypeStruct(x.shape, x.dtype) for x in carry],
        input_output_aliases={n_in + n_extra + k: n_out + k for k in range(n_carry)},
        scratch_shapes=scratch_shapes,
        compiler_params=pltpu.CompilerParams(vmem_limit_bytes=LIMIT),
        cost_estimate=LONGER,
    )(*args, *after, *carry)


def split_rows(row):
    high = row.astype(BF16).astype(F32)
    at = lax.broadcasted_iota(jnp.int32, (EXTRA, row.shape[-1]), 0)
    return jnp.where(at == 0, high, jnp.where(at == 1, row - high, 0.0)).astype(BF16)


def joined(ref):
    extra = ref[pl.ds(0, EXTRA), :].astype(F32)
    return extra[0:1] + extra[1:2]


def local_kernel(rows_ref, encw_ref, gain_ref, normed_ref, inverse_ref, encoded_ref):
    normed, inverse = normalised(rows_ref[...], encw_ref)
    normed_ref[...] = normed
    inverse_ref[...] = jnp.broadcast_to(inverse, inverse_ref.shape)
    encoded_ref[...] = (normed * gain_ref[...][None, :]).astype(BF16)


def finish_kernel(*refs):
    *grads, normed_ref, inverse_ref, gain_ref, mixed_ref, send_ref = refs
    grad = grads[0][...].astype(F32)
    for g in grads[1:]:
        grad = grad + g[...].astype(F32)
    normed = normed_ref[...]
    grad_normed = grad * gain_ref[...][None, :]
    grad_mixed = inverse_ref[...][:, :1] * (
        grad_normed - normed * jnp.mean(grad_normed * normed, axis=-1, keepdims=True)
    )
    mixed_ref[...] = grad_mixed
    send_ref[pl.ds(0, EXTRA), :] = split_rows(jnp.sum(grad * normed, axis=0, keepdims=True))
    send_ref[pl.ds(EXTRA, normed.shape[0]), :] = grad_mixed.astype(BF16)


def embed_kernel(mixed_ref, encw_ref, embed_ref):
    grad_mixed = mixed_ref[...]
    embed_ref[...] = (grad_mixed + mm_nt(grad_mixed.astype(BF16), encw_ref[...])).astype(BF16)


def outer_kernel(n_sec, where, *refs):
    rows_refs, gots, (keep_ref, give_ref, total) = refs[:n_sec], refs[n_sec:2 * n_sec], refs[2 * n_sec:]
    me, odd = where[0], where[1]
    part = rows_refs[0].shape[0]
    half = keep_ref.shape[0] - EXTRA
    own = 2 * half
    raw = jnp.concatenate([r[...] for r in rows_refs], axis=0)
    low = jnp.concatenate([g[pl.ds(EXTRA, part), :] for g in gots], axis=0)
    total[...] = mm_tn(raw, low)

    def rows_of(core):
        return total[pl.ds(pl.multiple_of(me * own + core * half, 8), half), :].astype(BF16)

    keep_ref[pl.ds(EXTRA, half), :] = rows_of(odd)
    give_ref[pl.ds(EXTRA, half), :] = rows_of(1 - odd)
    rows = [joined(g) for g in gots]
    gain_row = jnp.zeros_like(rows[0])
    for s in range(n_sec):
        for k in range(n_sec):
            here = lax.rem(me + n_sec - k, n_sec) == s
            gain_row = gain_row + jnp.where(here, rows[k], 0.0)
    extra = split_rows(gain_row)
    keep_ref[pl.ds(0, EXTRA), :] = extra
    give_ref[pl.ds(0, EXTRA), :] = extra


def merge_kernel(*refs):
    *ins, out_ref = refs
    half = out_ref.shape[0] - EXTRA
    gains = [joined(r) for r in ins]
    weights = [r[pl.ds(EXTRA, half), :].astype(F32) for r in ins]
    while len(gains) > 1:
        gains = [a + b for a, b in zip(gains[::2], gains[1::2])]
        weights = [a + b for a, b in zip(weights[::2], weights[1::2])]
    out_ref[pl.ds(0, EXTRA), :] = split_rows(gains[0])
    out_ref[pl.ds(EXTRA, half), :] = weights[0].astype(BF16)


def merged(*parts, **order):
    return call(merge_kernel, [(parts[0].shape, BF16)], *parts, **order)


def spread_kernel(where, own_ref, inc_ref, weight_ref, gain_ref):
    half = own_ref.shape[0] - EXTRA
    odd = where[1]
    for ref, at in ((own_ref, odd), (inc_ref, 1 - odd)):
        weight_ref[pl.ds(pl.multiple_of(at * half, 8), half), :] = ref[pl.ds(EXTRA, half), :].astype(F32)
    gain_ref[...] = joined(own_ref)[0]


def sum_kernel(plan, cut, where, *refs):
    n = len(plan)
    count = sum(arrays for arrays, _, _ in plan)
    sources, (out_ref, held, total, in_sems, out_sems) = refs[:count], refs[-5:]
    rows = out_ref.shape[0]
    size = rows // cut

    def fetch(k, c, which=0):
        start = sum(arrays for arrays, _, _ in plan[:k])
        block = plan[k][1]
        base = 0 if block is None else pl.multiple_of(where[block] * rows, rows)
        source = sources[start + which].at[pl.ds(base + c * size, size), :]
        return pltpu.make_async_copy(source, held.at[k, pl.ds(c * size, size), :], in_sems.at[k, c])

    def store(c):
        span = pl.ds(c * size, size)
        return pltpu.make_async_copy(total.at[span, :], out_ref.at[span, :], out_sems.at[c])

    for c in range(cut):
        for k, (arrays, _, choice) in enumerate(plan):
            if arrays == 1:
                fetch(k, c).start()
                continue
            for which in range(arrays):
                pl.when(where[choice] == which)(fetch(k, c, which).start)
    for c in range(cut):
        for k in range(n):
            fetch(k, c).wait()
        span = pl.ds(c * size, size)
        value = held[0, span, :].astype(F32)
        for k in range(1, n):
            value = value + held[k, span, :].astype(F32)
        total[span, :] = value.astype(total.dtype)
        store(c).start()
    for c in range(cut):
        store(c).wait()


def block_sum(rows, dtype, where, *terms, after=()):
    cut = 2 if rows % 32 == 0 else 1
    n = len(terms)
    sources = [x for arrays, _, _ in terms for x in arrays] + list(after)
    anywhere = pl.BlockSpec(memory_space=pl.ANY)
    return pl.pallas_call(
        functools.partial(sum_kernel, [(len(arrays), block, choice) for arrays, block, choice in terms], cut),
        in_specs=[pl.BlockSpec(memory_space=pltpu.SMEM)] + [anywhere] * len(sources),
        out_specs=anywhere,
        out_shape=jax.ShapeDtypeStruct((rows, ENC_D), dtype),
        scratch_shapes=[
            pltpu.VMEM((n, rows, ENC_D), BF16),
            pltpu.VMEM((rows, ENC_D), dtype),
            pltpu.SemaphoreType.DMA((n, cut)),
            pltpu.SemaphoreType.DMA((cut,)),
        ],
        compiler_params=pltpu.CompilerParams(vmem_limit_bytes=LIMIT),
        cost_estimate=SHORT,
    )(where, *sources)


def rotated(x, n, k):
    return lax.ppermute(x, "section", [(i, (i + k) % n) for i in range(n)]) if k else x


def chunk_at(chips, chip, step, core):
    place = jnp.where(core == 0, chip, chips - 1 - chip)
    ahead = jnp.minimum(chips - step + place, chips - 1)
    return jnp.where(core == 0, ahead, chips - 1 - ahead)


def body(n_sec, n_dp, nbr_embed, enc_weight, enc_gain, kv_weight, queries, pos_bias, nbr_ids, ctx_grad):
    local_rows = nbr_embed[0].reshape(-1, ENC_D)
    part = local_rows.shape[0]
    own = ENC_D // n_sec
    half = own // 2
    chips = n_dp // 2
    kv_rows = 2 * HEADS * HEAD // n_dp
    me = lax.axis_index("section")
    rank = lax.axis_index("dp")
    chip, core = rank // 2, lax.rem(rank, 2)
    near = [(i, i ^ 1) for i in range(n_dp)]

    early = chips // 2
    where, places = [me, core], {}

    def place(name, chunk, lane):
        keyed = chunk < chips // 2
        spot = jnp.where(keyed, chunk, chips - 1 - chunk)
        mine = jnp.where(keyed, core, 1 - core)
        places[name] = range(len(where), len(where) + 3)
        where.extend([2 * spot + lane, mine, 1 - mine])

    for step in range(1, chips):
        for j, lane in enumerate((1 - core, core)):
            place((step, j), chunk_at(chips, chip, step, core), lane)
    place("other", chip, 1 - core)
    place("own", chip, core)
    where = jnp.stack(where).astype(jnp.int32)
    spot = jnp.stack([me, core]).astype(jnp.int32)

    rows = [rotated(local_rows, n_sec, k) for k in range(n_sec)]
    normed, inverse, encoded = call(
        local_kernel,
        [((part, ENC_D), F32), ((part, HEAD), F32), ((part, ENC_D), BF16)],
        local_rows, enc_weight, enc_gain, after=[spot],
    )
    grad_query, first, second, *grad_enc = layer(
        n_sec, chips, nbr_ids[0], where, [encoded] + rows[1:], enc_weight, enc_gain, kv_weight[0], queries[0], pos_bias[0], ctx_grad[0]
    )
    got = [rotated(grad_enc[k], n_sec, k) for k in range(n_sec)]
    incoming = [None, None]
    state = {"where": where, "sums": []}
    mine = [first, second]
    theirs = [lax.ppermute(x, "dp", near) for x in mine]

    def kv_step(step, lanes=(0, 1)):
        hops = [(2 * a, 2 * a + 2) for a in range(step)]
        hops += [(2 * (chips - 1 - a) + 1, 2 * (chips - 2 - a) + 1) for a in range(step)]
        for j in lanes:
            block, here, there = places[step, j]
            if step <= early:
                terms = [(mine[1:], block, None), (theirs[:1], block, None)]
            else:
                terms = [(mine, block, here), (theirs, block, there)]
            if incoming[j] is not None:
                terms.append(([incoming[j]], None, None))
            out = block_sum(kv_rows, BF16, state["where"], *terms, after=state["sums"][-j:] if j else ())
            incoming[j] = lax.ppermute(out, "dp", hops)
            state["sums"].append(out)

    def last_pair():
        block, here, _ = places["other"]
        out = block_sum(kv_rows, BF16, state["where"], (mine, block, here), ([incoming[0]], None, None))
        state["swapped"] = lax.ppermute(out, "dp", near)
        state["sums"].append(out)

    def order():
        sums, state["sums"] = state["sums"], []
        return {"after": sums, "carry": [state["where"]]}

    def finish_stage():
        held = order()
        held["after"] = held["after"] + theirs[1:]
        state["mixed"], send, state["where"] = call(
            finish_kernel,
            [((part, ENC_D), F32), ((EXTRA + part, ENC_D), BF16)],
            *got, normed, inverse, enc_gain, **held,
        )
        state["lows"] = [rotated(send, n_sec, k) for k in range(n_sec)]

    def outer_stage():
        shape = ((EXTRA + half, ENC_D), BF16)
        *state["halves"], state["where"] = call(
            functools.partial(outer_kernel, n_sec),
            [shape, shape],
            spot, *rows, *state["lows"],
            scalars=1,
            scratch_shapes=[pltpu.VMEM((ENC_D, ENC_D), F32)],
            **order(),
        )

    def swap(x, dist):
        return lax.ppermute(x, "dp", [(i, i ^ dist) for i in range(n_dp)])

    def pair_stage():
        keep, give = state["halves"]
        state["payload"], state["where"] = merged(keep, swap(give, 1), **order())

    def embed_stage():
        (state["embed"],) = call(embed_kernel, [((part, ENC_D), BF16)], state["mixed"], enc_weight, after=[state["payload"]])

    def merge_stage(dist):
        payload = state["payload"]
        state["payload"], state["where"] = merged(payload, swap(payload, dist), **order())

    merges = [functools.partial(merge_stage, 2 << k) for k in range((chips - 1).bit_length())]
    enc_chain = [finish_stage, outer_stage, pair_stage] + merges
    kv_chain = [functools.partial(kv_step, step) for step in range(1, min(chips, 3))]
    kv_chain += [functools.partial(kv_step, step, (j,)) for step in range(3, chips) for j in range(2)] + [last_pair]
    for at in range(max(len(kv_chain), len(enc_chain))):
        for chain in (kv_chain, enc_chain):
            if at < len(chain):
                chain[at]()
        if at == 3:
            embed_stage()
    payload = state["payload"]
    other = lax.ppermute(payload, "dp", near)
    weight_grad, gain_row, table = call(
        spread_kernel, [((own, ENC_D), F32), ((ENC_D,), F32)], spot, payload, other,
        scalars=1, **order(),
    )
    block, here, _ = places["own"]
    kv_grad = block_sum(
        kv_rows, F32, table, (mine, block, here), ([state["swapped"]], None, None), ([incoming[1]], None, None)
    )
    embed_grad = state["embed"]
    return (
        grad_query[None],
        kv_grad[None],
        weight_grad,
        gain_row,
        embed_grad.reshape(nbr_embed.shape),
    )


def solution(mesh):
    return jax.shard_map(
        functools.partial(body, mesh.shape["section"], mesh.shape["dp"]),
        mesh=mesh,
        in_specs=(
            P("dp", None, "section", None),
            P(),
            P(),
            P("section", None, None),
            P("section", "dp", None),
            P("section", None, None, None),
            P("dp", None, None),
            P("section", "dp", None),
        ),
        out_specs=(
            P("section", "dp", None),
            P("section", "dp", None),
            P("section", None),
            P(),
            P("dp", None, "section", None),
        ),
        check_vma=False,
    )
```

```python
import functools
import math

import jax
import jax.numpy as jnp
from jax import lax
from jax.experimental import pallas as pl
from jax.experimental.pallas import tpu as pltpu
from jax.sharding import PartitionSpec as P

HEADS = 16
HEAD = 128
ENC_D = 896
BLOCK = 64
NBR = 2
NLEN = 128
TOK_DEV = 128
NSET = 4
PAIR = 2
STEP = 4
EXTRA = 16

eps_norm = 1e-06
LIMIT = 65400 * 1024
SHORT = pl.CostEstimate(flops=1, bytes_accessed=1, transcendentals=0)
LONGER = pl.CostEstimate(flops=20_000_000_000, bytes_accessed=1_000_000, transcendentals=0)
F32 = jnp.float32
BF16 = jnp.bfloat16


def mm(a, b):
    return lax.dot_general(a, b, (((1,), (0,)), ((), ())), preferred_element_type=F32)


def mm_nt(a, b):
    return lax.dot_general(a, b, (((1,), (1,)), ((), ())), preferred_element_type=F32)


def mm_tn(a, b):
    return lax.dot_general(a, b, (((0,), (0,)), ((), ())), preferred_element_type=F32)


def chunk_order(chips, width):
    rows = 2 * HEADS * HEAD // chips
    return max(1, rows // width), max(1, width // rows)


def normalised(raw, encw_ref):
    mixed = raw.astype(F32) + mm(raw, encw_ref[...])
    inverse = lax.rsqrt(jnp.mean(mixed * mixed, axis=-1, keepdims=True) + eps_norm)
    return mixed * inverse, inverse


def layer_kernel(
    n_sec, chips, ids, where, *refs,
):
    rows_refs, (encw_ref, gain_ref, w_ref, q_ref, bias_ref, up_ref) = refs[:n_sec], refs[n_sec:n_sec + 6]
    qg_ref, first_ref, second_ref, *rest = refs[n_sec + 6:]
    ge_refs, (enc, proj, total, gset, acc) = rest[:n_sec], rest[n_sec:]
    step = pl.program_id(0)
    part = NLEN // n_sec
    blocks = TOK_DEV // BLOCK
    width = STEP * HEAD
    factor = 1.0 / math.sqrt(HEAD)

    @pl.when(step == 0)
    def _():
        def places(k):
            s = lax.rem(where[0] + n_sec - k, n_sec)
            return [(e, pl.ds(pl.multiple_of(e * NLEN + s * part, part), part)) for e in range(NSET)]

        others = jnp.concatenate([r[...] for r in rows_refs[1:]], axis=0)
        normed, _ = normalised(others, encw_ref)
        encoded = (normed * gain_ref[...][None, :]).astype(BF16)
        for e, span in places(0):
            enc[span, :] = rows_refs[0][pl.ds(e * part, part), :]
        for k in range(1, n_sec):
            for e, span in places(k):
                at = ((k - 1) * NSET + e) * part
                enc[span, :] = encoded[at:at + part]
        acc[...] = jnp.zeros_like(acc)

    encoded = enc[...]
    weights = w_ref[...].reshape(2 * width, ENC_D)
    proj[...] = mm_nt(encoded, weights).astype(BF16)
    total[...] = jnp.zeros_like(total)
    spans = [
        [pl.ds(pl.multiple_of(ids[c, n] * NLEN, NLEN), NLEN) for n in range(NBR)]
        for c in range(blocks)
    ]
    toks = [slice(c * BLOCK, (c + 1) * BLOCK) for c in range(blocks)]
    pair = PAIR * HEAD
    items = [(c, g) for c in range(blocks) for g in range(STEP // PAIR)]

    def stacked(ref, c, g):
        x = ref[toks[c], g * pair:(g + 1) * pair]
        head_of = lax.broadcasted_iota(jnp.int32, x.shape, 1) // HEAD
        return jnp.concatenate([jnp.where(head_of == h, x, jnp.zeros_like(x)) for h in range(PAIR)], axis=0)

    def picked(c, g, base):
        return jnp.concatenate([proj[s, base + g * pair:base + (g + 1) * pair] for s in spans[c]], axis=0)

    def bias(g):
        return jnp.concatenate([bias_ref[g * PAIR + h] for h in range(PAIR)], axis=0).astype(F32)

    keys = {i: picked(*i, 0) for i in items}
    values = {i: picked(*i, width) for i in items}
    query = {i: stacked(q_ref, *i) for i in items}
    upstream = {i: stacked(up_ref, *i) for i in items}
    scores = {i: mm_nt(query[i], keys[i]) * factor + bias(i[1]) for i in items}
    dprobs = {i: mm_nt(upstream[i], values[i]) for i in items}
    exps = {i: jnp.exp(scores[i] - jnp.max(scores[i], axis=-1, keepdims=True)) for i in items}
    probs = {i: exps[i] / jnp.sum(exps[i], axis=-1, keepdims=True) for i in items}
    dvalues = {i: mm_tn(probs[i].astype(BF16), upstream[i]) for i in items}
    inner = {i: jnp.sum(probs[i] * dprobs[i], axis=-1, keepdims=True) for i in items}
    dscores = {i: (probs[i] * (dprobs[i] - inner[i])).astype(BF16) for i in items}
    dkeys = {i: mm_tn(dscores[i], query[i]) * factor for i in items}
    dquery = {i: mm(dscores[i], keys[i]) * factor for i in items}
    for c, g in items:
        for h in range(PAIR):
            col = slice(h * HEAD, (h + 1) * HEAD)
            qg_ref[toks[c], g * pair + h * HEAD:g * pair + (h + 1) * HEAD] = (
                dquery[c, g][h * BLOCK:(h + 1) * BLOCK, col].astype(BF16)
            )
        for n, s in enumerate(spans[c]):
            total[s, g * pair:(g + 1) * pair] += dkeys[c, g][n * NLEN:(n + 1) * NLEN]
            total[s, width + g * pair:width + (g + 1) * pair] += dvalues[c, g][n * NLEN:(n + 1) * NLEN]
    gset[...] = total[...].astype(BF16)
    acc[...] += mm(gset[...], weights)
    kv = mm_tn(gset[...], encoded).astype(BF16)
    keys_part, values_part = kv[:width], kv[width:]
    _, inside = chunk_order(chips, width)
    size = width // inside
    values_part = jnp.concatenate([values_part[u * size:(u + 1) * size] for u in reversed(range(inside))], axis=0)
    low = where[1] == 0
    first_ref[...] = jnp.where(low, keys_part, values_part)
    second_ref[...] = jnp.where(low, values_part, keys_part)

    @pl.when(step == pl.num_programs(0) - 1)
    def _():
        for k in range(n_sec):
            s = lax.rem(where[0] + k, n_sec)
            for e in range(NSET):
                span = pl.ds(pl.multiple_of(e * NLEN + s * part, part), part)
                ge_refs[k][pl.ds(e * part, part), :] = acc[span, :].astype(BF16)


def layer(n_sec, chips, ids, where, rows, enc_weight, gain, weights, queries, bias, upstream):
    head_width = HEADS * HEAD
    width = STEP * HEAD
    steps = HEADS // STEP
    all_rows = NSET * NLEN
    part = all_rows // n_sec
    blocks, _ = chunk_order(chips, width)

    def half(core):
        def at(i, ids, where):
            turned = (steps // blocks - 1 - i // blocks) * blocks + lax.rem(i, blocks)
            return jnp.where(where[1] == core, i, turned), 0

        return pl.BlockSpec((width, ENC_D), at)

    fixed2 = lambda i, *_: (0, 0)
    fixed3 = lambda i, *_: (0, 0, 0)
    return pl.pallas_call(
        functools.partial(layer_kernel, n_sec, chips),
        grid_spec=pltpu.PrefetchScalarGridSpec(
            num_scalar_prefetch=2,
            grid=(steps,),
            in_specs=[
                *[pl.BlockSpec((part, ENC_D), fixed2)] * n_sec,
                pl.BlockSpec((ENC_D, ENC_D), fixed2),
                pl.BlockSpec((ENC_D,), lambda i, *_: (0,)),
                pl.BlockSpec((2, width, ENC_D), lambda i, *_: (0, i, 0)),
                pl.BlockSpec((TOK_DEV, width), lambda i, *_: (0, i)),
                pl.BlockSpec((STEP, BLOCK, NBR * NLEN), lambda i, *_: (i, 0, 0)),
                pl.BlockSpec((TOK_DEV, width), lambda i, *_: (0, i)),
            ],
            out_specs=[
                pl.BlockSpec((TOK_DEV, width), lambda i, *_: (0, i)),
                half(0),
                half(1),
            ]
            + [pl.BlockSpec((part, ENC_D), fixed2)] * n_sec,
            scratch_shapes=[
                pltpu.VMEM((all_rows, ENC_D), BF16),
                pltpu.VMEM((all_rows, 2 * width), BF16),
                pltpu.VMEM((all_rows, 2 * width), F32),
                pltpu.VMEM((all_rows, 2 * width), BF16),
                pltpu.VMEM((all_rows, ENC_D), F32),
            ],
        ),
        out_shape=[
            jax.ShapeDtypeStruct((TOK_DEV, head_width), BF16),
            jax.ShapeDtypeStruct((head_width, ENC_D), BF16),
            jax.ShapeDtypeStruct((head_width, ENC_D), BF16),
        ]
        + [jax.ShapeDtypeStruct((part, ENC_D), BF16)] * n_sec,
        compiler_params=pltpu.CompilerParams(
            vmem_limit_bytes=LIMIT, dimension_semantics=("arbitrary",)
        ),
        cost_estimate=SHORT,
    )(ids, where, *rows, enc_weight, gain, weights.reshape(2, head_width, ENC_D), queries, bias, upstream)


def call(kernel, outs, *args, after=(), carry=(), scalars=0, scratch_shapes=(), cost=LONGER):
    n_in, n_out, n_extra, n_carry = len(args), len(outs), len(after), len(carry)

    def inner(*refs):
        own = refs[n_in + n_extra + n_carry:]
        kernel(*refs[:n_in], *own[:n_out], *own[n_out + n_carry:])

    vmem, anywhere = pl.BlockSpec(memory_space=pltpu.VMEM), pl.BlockSpec(memory_space=pl.ANY)
    return pl.pallas_call(
        inner,
        in_specs=[pl.BlockSpec(memory_space=pltpu.SMEM)] * scalars
        + [vmem] * (n_in - scalars)
        + [anywhere] * (n_extra + n_carry),
        out_specs=[vmem] * n_out + [anywhere] * n_carry,
        out_shape=[jax.ShapeDtypeStruct(shape, dtype) for shape, dtype in outs]
        + [jax.ShapeDtypeStruct(x.shape, x.dtype) for x in carry],
        input_output_aliases={n_in + n_extra + k: n_out + k for k in range(n_carry)},
        scratch_shapes=scratch_shapes,
        compiler_params=pltpu.CompilerParams(vmem_limit_bytes=LIMIT),
        cost_estimate=cost,
    )(*args, *after, *carry)


def split_rows(row):
    high = row.astype(BF16).astype(F32)
    at = lax.broadcasted_iota(jnp.int32, (EXTRA, row.shape[-1]), 0)
    return jnp.where(at == 0, high, jnp.where(at == 1, row - high, 0.0)).astype(BF16)


def joined(ref):
    extra = ref[pl.ds(0, EXTRA), :].astype(F32)
    return extra[0:1] + extra[1:2]


def local_kernel(rows_ref, encw_ref, gain_ref, normed_ref, inverse_ref, encoded_ref):
    normed, inverse = normalised(rows_ref[...], encw_ref)
    normed_ref[...] = normed
    inverse_ref[...] = jnp.broadcast_to(inverse, inverse_ref.shape)
    encoded_ref[...] = (normed * gain_ref[...][None, :]).astype(BF16)


def finish_kernel(*refs):
    *grads, normed_ref, inverse_ref, gain_ref, mixed_ref, send_ref = refs
    grad = grads[0][...].astype(F32)
    for g in grads[1:]:
        grad = grad + g[...].astype(F32)
    normed = normed_ref[...]
    grad_normed = grad * gain_ref[...][None, :]
    grad_mixed = inverse_ref[...][:, :1] * (
        grad_normed - normed * jnp.mean(grad_normed * normed, axis=-1, keepdims=True)
    )
    mixed_ref[...] = grad_mixed
    send_ref[pl.ds(0, EXTRA), :] = split_rows(jnp.sum(grad * normed, axis=0, keepdims=True))
    send_ref[pl.ds(EXTRA, normed.shape[0]), :] = grad_mixed.astype(BF16)


def embed_kernel(mixed_ref, encw_ref, embed_ref):
    grad_mixed = mixed_ref[...]
    embed_ref[...] = (grad_mixed + mm_nt(grad_mixed.astype(BF16), encw_ref[...])).astype(BF16)


def outer_kernel(n_sec, where, *refs):
    rows_refs, gots, (keep_ref, give_ref, total) = refs[:n_sec], refs[n_sec:2 * n_sec], refs[2 * n_sec:]
    me, odd = where[0], where[1]
    part = rows_refs[0].shape[0]
    half = keep_ref.shape[0] - EXTRA
    own = 2 * half
    raw = jnp.concatenate([r[...] for r in rows_refs], axis=0)
    low = jnp.concatenate([g[pl.ds(EXTRA, part), :] for g in gots], axis=0)
    total[...] = mm_tn(raw, low)

    def rows_of(core):
        return total[pl.ds(pl.multiple_of(me * own + core * half, 8), half), :].astype(BF16)

    keep_ref[pl.ds(EXTRA, half), :] = rows_of(odd)
    give_ref[pl.ds(EXTRA, half), :] = rows_of(1 - odd)
    rows = [joined(g) for g in gots]
    gain_row = jnp.zeros_like(rows[0])
    for s in range(n_sec):
        for k in range(n_sec):
            here = lax.rem(me + n_sec - k, n_sec) == s
            gain_row = gain_row + jnp.where(here, rows[k], 0.0)
    extra = split_rows(gain_row)
    keep_ref[pl.ds(0, EXTRA), :] = extra
    give_ref[pl.ds(0, EXTRA), :] = extra


def merge_kernel(*refs):
    *ins, out_ref = refs
    half = out_ref.shape[0] - EXTRA
    gains = [joined(r) for r in ins]
    weights = [r[pl.ds(EXTRA, half), :].astype(F32) for r in ins]
    while len(gains) > 1:
        gains = [a + b for a, b in zip(gains[::2], gains[1::2])]
        weights = [a + b for a, b in zip(weights[::2], weights[1::2])]
    out_ref[pl.ds(0, EXTRA), :] = split_rows(gains[0])
    out_ref[pl.ds(EXTRA, half), :] = weights[0].astype(BF16)


def merged(*parts, **order):
    return call(merge_kernel, [(parts[0].shape, BF16)], *parts, **order)


def spread_kernel(where, own_ref, inc_ref, weight_ref, gain_ref):
    half = own_ref.shape[0] - EXTRA
    odd = where[1]
    for ref, at in ((own_ref, odd), (inc_ref, 1 - odd)):
        weight_ref[pl.ds(pl.multiple_of(at * half, 8), half), :] = ref[pl.ds(EXTRA, half), :].astype(F32)
    gain_ref[...] = joined(own_ref)[0]


def sum_kernel(plan, cut, where, *refs):
    n = len(plan)
    count = sum(arrays for arrays, _, _ in plan)
    sources, (out_ref, held, total, in_sems, out_sems) = refs[:count], refs[-5:]
    rows = out_ref.shape[0]
    size = rows // cut

    def fetch(k, c, which=0):
        start = sum(arrays for arrays, _, _ in plan[:k])
        block = plan[k][1]
        base = 0 if block is None else pl.multiple_of(where[block] * rows, rows)
        source = sources[start + which].at[pl.ds(base + c * size, size), :]
        return pltpu.make_async_copy(source, held.at[k, pl.ds(c * size, size), :], in_sems.at[k, c])

    def store(c):
        span = pl.ds(c * size, size)
        return pltpu.make_async_copy(total.at[span, :], out_ref.at[span, :], out_sems.at[c])

    for c in range(cut):
        for k, (arrays, _, choice) in enumerate(plan):
            if arrays == 1:
                fetch(k, c).start()
                continue
            for which in range(arrays):
                pl.when(where[choice] == which)(fetch(k, c, which).start)
    for c in range(cut):
        for k in range(n):
            fetch(k, c).wait()
        span = pl.ds(c * size, size)
        value = held[0, span, :].astype(F32)
        for k in range(1, n):
            value = value + held[k, span, :].astype(F32)
        total[span, :] = value.astype(total.dtype)
        store(c).start()
    for c in range(cut):
        store(c).wait()


def block_sum(rows, dtype, where, *terms, after=()):
    cut = (4 if dtype == F32 else 2) if rows % 64 == 0 else 1
    n = len(terms)
    sources = [x for arrays, _, _ in terms for x in arrays] + list(after)
    anywhere = pl.BlockSpec(memory_space=pl.ANY)
    return pl.pallas_call(
        functools.partial(sum_kernel, [(len(arrays), block, choice) for arrays, block, choice in terms], cut),
        in_specs=[pl.BlockSpec(memory_space=pltpu.SMEM)] + [anywhere] * len(sources),
        out_specs=anywhere,
        out_shape=jax.ShapeDtypeStruct((rows, ENC_D), dtype),
        scratch_shapes=[
            pltpu.VMEM((n, rows, ENC_D), BF16),
            pltpu.VMEM((rows, ENC_D), dtype),
            pltpu.SemaphoreType.DMA((n, cut)),
            pltpu.SemaphoreType.DMA((cut,)),
        ],
        compiler_params=pltpu.CompilerParams(vmem_limit_bytes=LIMIT),
        cost_estimate=SHORT,
    )(where, *sources)


def rotated(x, n, k):
    return lax.ppermute(x, "section", [(i, (i + k) % n) for i in range(n)]) if k else x


def chunk_at(chips, chip, step, core):
    place = jnp.where(core == 0, chip, chips - 1 - chip)
    ahead = jnp.minimum(chips - step + place, chips - 1)
    return jnp.where(core == 0, ahead, chips - 1 - ahead)


def body(n_sec, n_dp, nbr_embed, enc_weight, enc_gain, kv_weight, queries, pos_bias, nbr_ids, ctx_grad):
    local_rows = nbr_embed[0].reshape(-1, ENC_D)
    part = local_rows.shape[0]
    own = ENC_D // n_sec
    half = own // 2
    chips = n_dp // 2
    kv_rows = 2 * HEADS * HEAD // n_dp
    me = lax.axis_index("section")
    rank = lax.axis_index("dp")
    chip, core = rank // 2, lax.rem(rank, 2)
    near = [(i, i ^ 1) for i in range(n_dp)]

    early = chips // 2
    where, places = [me, core], {}

    def place(name, chunk, lane):
        keyed = chunk < chips // 2
        spot = jnp.where(keyed, chunk, chips - 1 - chunk)
        mine = jnp.where(keyed, core, 1 - core)
        places[name] = range(len(where), len(where) + 3)
        where.extend([2 * spot + lane, mine, 1 - mine])

    for step in range(1, chips):
        for j, lane in enumerate((1 - core, core)):
            place((step, j), chunk_at(chips, chip, step, core), lane)
    place("other", chip, 1 - core)
    place("own", chip, core)
    where = jnp.stack(where).astype(jnp.int32)
    spot = jnp.stack([me, core]).astype(jnp.int32)

    rows = [rotated(local_rows, n_sec, k) for k in range(n_sec)]
    normed, inverse, encoded = call(
        local_kernel,
        [((part, ENC_D), F32), ((part, HEAD), F32), ((part, ENC_D), BF16)],
        local_rows, enc_weight, enc_gain, after=[spot],
    )
    grad_query, first, second, *grad_enc = layer(
        n_sec, chips, nbr_ids[0], where, [encoded] + rows[1:], enc_weight, enc_gain, kv_weight[0], queries[0], pos_bias[0], ctx_grad[0]
    )
    got = [rotated(grad_enc[k], n_sec, k) for k in range(n_sec)]
    incoming = [None, None]
    state = {"where": where, "sums": []}
    mine = [first, second]
    theirs = [lax.ppermute(x, "dp", near) for x in mine]

    def kv_step(step, lanes=(0, 1)):
        hops = [(2 * a, 2 * a + 2) for a in range(step)]
        hops += [(2 * (chips - 1 - a) + 1, 2 * (chips - 2 - a) + 1) for a in range(step)]
        for j in lanes:
            block, here, there = places[step, j]
            if step <= early:
                terms = [(mine[1:], block, None), (theirs[:1], block, None)]
            else:
                terms = [(mine, block, here), (theirs, block, there)]
            if incoming[j] is not None:
                terms.append(([incoming[j]], None, None))
            out = block_sum(kv_rows, BF16, state["where"], *terms, after=state["sums"][-j:] if j else ())
            incoming[j] = lax.ppermute(out, "dp", hops)
            state["sums"].append(out)

    def last_pair():
        block, here, _ = places["other"]
        terms = [(mine, block, here), ([incoming[0]], None, None)]
        out = block_sum(kv_rows, BF16, state["where"], *terms)
        state["swapped"] = lax.ppermute(out, "dp", near)
        state["sums"].append(out)

    def order():
        sums, state["sums"] = state["sums"], []
        return {"after": sums, "carry": [state["where"]]}

    def finish_stage():
        held = order()
        held["after"] = held["after"] + theirs[1:]
        state["mixed"], send, state["where"] = call(
            finish_kernel,
            [((part, ENC_D), F32), ((EXTRA + part, ENC_D), BF16)],
            *got, normed, inverse, enc_gain, **held,
        )
        state["lows"] = [rotated(send, n_sec, k) for k in range(n_sec)]

    def outer_stage():
        shape = ((EXTRA + half, ENC_D), BF16)
        *state["halves"], state["where"] = call(
            functools.partial(outer_kernel, n_sec),
            [shape, shape],
            spot, *rows, *state["lows"],
            scalars=1,
            scratch_shapes=[pltpu.VMEM((ENC_D, ENC_D), F32)],
            **order(),
        )

    def swap(x, dist):
        return lax.ppermute(x, "dp", [(i, i ^ dist) for i in range(n_dp)])

    def pair_stage():
        keep, give = state["halves"]
        state["payload"], state["where"] = merged(keep, swap(give, 1), cost=SHORT, **order())

    def embed_stage():
        (state["embed"],) = call(embed_kernel, [((part, ENC_D), BF16)], state["mixed"], enc_weight, after=[state["payload"]], cost=LONGER)

    def merge_stage(dist):
        payload = state["payload"]
        state["payload"], state["where"] = merged(payload, swap(payload, dist), cost=LONGER if dist == 2 else LONGER, **order())

    merges = [functools.partial(merge_stage, 2 << k) for k in range((chips - 1).bit_length())]
    enc_chain = [finish_stage, outer_stage, pair_stage] + merges
    kv_chain = [functools.partial(kv_step, step) for step in range(1, min(chips, 3))]
    kv_chain += [functools.partial(kv_step, step, (j,)) for step in range(3, chips) for j in range(2)] + [last_pair]
    for at in range(max(len(kv_chain), len(enc_chain))):
        for chain in (kv_chain, enc_chain):
            if at < len(chain):
                chain[at]()
        if at == 3:
            embed_stage()
    payload = state["payload"]
    other = lax.ppermute(payload, "dp", near)
    held = order()
    weight_grad, gain_row, table = call(
        spread_kernel, [((own, ENC_D), F32), ((ENC_D,), F32)], spot, payload, other, scalars=1, cost=LONGER, **held,
    )
    block, here, _ = places["own"]
    kv_grad = block_sum(
        kv_rows, F32, table, (mine, block, here), ([state["swapped"]], None, None), ([incoming[1]], None, None)
    )
    embed_grad = state["embed"]
    return (
        grad_query[None],
        kv_grad[None],
        weight_grad,
        gain_row,
        embed_grad.reshape(nbr_embed.shape),
    )


def solution(mesh):
    return jax.shard_map(
        functools.partial(body, mesh.shape["section"], mesh.shape["dp"]),
        mesh=mesh,
        in_specs=(
            P("dp", None, "section", None),
            P(),
            P(),
            P("section", None, None),
            P("section", "dp", None),
            P("section", None, None, None),
            P("dp", None, None),
            P("section", "dp", None),
        ),
        out_specs=(
            P("section", "dp", None),
            P("section", "dp", None),
            P("section", None),
            P(),
            P("dp", None, "section", None),
        ),
        check_vma=False,
    )
```

```python
import functools
import math

import jax
import jax.numpy as jnp
from jax import lax
from jax.experimental import pallas as pl
from jax.experimental.pallas import tpu as pltpu
from jax.sharding import PartitionSpec as P

HEADS = 16
HEAD = 128
ENC_D = 896
BLOCK = 64
NBR = 2
NLEN = 128
TOK_DEV = 128
NSET = 4
PAIR = 2
STEP = 4
EXTRA = 16

eps_norm = 1e-06
LIMIT = 65400 * 1024
SHORT = pl.CostEstimate(flops=1, bytes_accessed=1, transcendentals=0)
LONGER = pl.CostEstimate(flops=20_000_000_000, bytes_accessed=1_000_000, transcendentals=0)
F32 = jnp.float32
BF16 = jnp.bfloat16


def mm(a, b):
    return lax.dot_general(a, b, (((1,), (0,)), ((), ())), preferred_element_type=F32)


def mm_nt(a, b):
    return lax.dot_general(a, b, (((1,), (1,)), ((), ())), preferred_element_type=F32)


def mm_tn(a, b):
    return lax.dot_general(a, b, (((0,), (0,)), ((), ())), preferred_element_type=F32)


def chunk_order(chips, width):
    rows = 2 * HEADS * HEAD // chips
    return max(1, rows // width), max(1, width // rows)


def normalised(raw, encw_ref):
    mixed = raw.astype(F32) + mm(raw, encw_ref[...])
    inverse = lax.rsqrt(jnp.mean(mixed * mixed, axis=-1, keepdims=True) + eps_norm)
    return mixed * inverse, inverse


def layer_kernel(
    n_sec, chips, ids, where, *refs,
):
    rows_refs, (encw_ref, gain_ref, w_ref, q_ref, bias_ref, up_ref) = refs[:n_sec], refs[n_sec:n_sec + 6]
    qg_ref, first_ref, second_ref, *rest = refs[n_sec + 6:]
    ge_refs, (enc, proj, total, gset, acc) = rest[:n_sec], rest[n_sec:]
    step = pl.program_id(0)
    part = NLEN // n_sec
    blocks = TOK_DEV // BLOCK
    width = STEP * HEAD
    factor = 1.0 / math.sqrt(HEAD)

    @pl.when(step == 0)
    def _():
        def places(k):
            s = lax.rem(where[0] + n_sec - k, n_sec)
            return [(e, pl.ds(pl.multiple_of(e * NLEN + s * part, part), part)) for e in range(NSET)]

        others = jnp.concatenate([r[...] for r in rows_refs[1:]], axis=0)
        normed, _ = normalised(others, encw_ref)
        encoded = (normed * gain_ref[...][None, :]).astype(BF16)
        for e, span in places(0):
            enc[span, :] = rows_refs[0][pl.ds(e * part, part), :]
        for k in range(1, n_sec):
            for e, span in places(k):
                at = ((k - 1) * NSET + e) * part
                enc[span, :] = encoded[at:at + part]
        acc[...] = jnp.zeros_like(acc)

    encoded = enc[...]
    weights = w_ref[...].reshape(2 * width, ENC_D)
    proj[...] = mm_nt(encoded, weights).astype(BF16)
    spans = [
        [pl.ds(pl.multiple_of(ids[c, n] * NLEN, NLEN), NLEN) for n in range(NBR)]
        for c in range(blocks)
    ]
    toks = [slice(c * BLOCK, (c + 1) * BLOCK) for c in range(blocks)]
    pair = PAIR * HEAD
    items = [(c, g) for c in range(blocks) for g in range(STEP // PAIR)]

    def stacked(ref, c, g):
        x = ref[toks[c], g * pair:(g + 1) * pair]
        head_of = lax.broadcasted_iota(jnp.int32, x.shape, 1) // HEAD
        return jnp.concatenate([jnp.where(head_of == h, x, jnp.zeros_like(x)) for h in range(PAIR)], axis=0)

    def picked(c, g, base):
        return jnp.concatenate([proj[s, base + g * pair:base + (g + 1) * pair] for s in spans[c]], axis=0)

    def bias(g):
        return jnp.concatenate([bias_ref[g * PAIR + h] for h in range(PAIR)], axis=0).astype(F32)

    keys = {i: picked(*i, 0) for i in items}
    values = {i: picked(*i, width) for i in items}
    query = {i: stacked(q_ref, *i) for i in items}
    upstream = {i: stacked(up_ref, *i) for i in items}
    scores = {i: mm_nt(query[i], keys[i]) * factor + bias(i[1]) for i in items}
    dprobs = {i: mm_nt(upstream[i], values[i]) for i in items}
    exps = {i: jnp.exp(scores[i] - jnp.max(scores[i], axis=-1, keepdims=True)) for i in items}
    probs = {i: exps[i] / jnp.sum(exps[i], axis=-1, keepdims=True) for i in items}
    dvalues = {i: mm_tn(probs[i].astype(BF16), upstream[i]) for i in items}
    inner = {i: jnp.sum(probs[i] * dprobs[i], axis=-1, keepdims=True) for i in items}
    dscores = {i: (probs[i] * (dprobs[i] - inner[i])).astype(BF16) for i in items}
    dkeys = {i: mm_tn(dscores[i], query[i]) * factor for i in items}
    dquery = {i: mm(dscores[i], keys[i]) * factor for i in items}
    for c, g in items:
        for h in range(PAIR):
            col = slice(h * HEAD, (h + 1) * HEAD)
            qg_ref[toks[c], g * pair + h * HEAD:g * pair + (h + 1) * HEAD] = (
                dquery[c, g][h * BLOCK:(h + 1) * BLOCK, col].astype(BF16)
            )
        for base, grads in ((0, dkeys[c, g]), (width, dvalues[c, g])):
            cols = slice(base + g * pair, base + (g + 1) * pair)
            parts = [grads[n * NLEN:(n + 1) * NLEN] for n in range(NBR)]
            if c > 0:
                for n, s in enumerate(spans[c]):
                    total[s, cols] += parts[n]
                continue
            for e in range(NSET):
                picked_parts = [jnp.where(ids[c, n] == e, parts[n], 0.0) for n in range(NBR)]
                total[e * NLEN:(e + 1) * NLEN, cols] = sum(picked_parts[1:], picked_parts[0])
    gset[...] = total[...].astype(BF16)
    acc[...] += mm(gset[...], weights)
    kv = mm_tn(gset[...], encoded).astype(BF16)
    keys_part, values_part = kv[:width], kv[width:]
    _, inside = chunk_order(chips, width)
    size = width // inside
    values_part = jnp.concatenate([values_part[u * size:(u + 1) * size] for u in reversed(range(inside))], axis=0)
    low = where[1] == 0
    first_ref[...] = jnp.where(low, keys_part, values_part)
    second_ref[...] = jnp.where(low, values_part, keys_part)

    @pl.when(step == pl.num_programs(0) - 1)
    def _():
        for k in range(n_sec):
            s = lax.rem(where[0] + k, n_sec)
            for e in range(NSET):
                span = pl.ds(pl.multiple_of(e * NLEN + s * part, part), part)
                ge_refs[k][pl.ds(e * part, part), :] = acc[span, :].astype(BF16)


def layer(n_sec, chips, ids, where, rows, enc_weight, gain, weights, queries, bias, upstream):
    head_width = HEADS * HEAD
    width = STEP * HEAD
    steps = HEADS // STEP
    all_rows = NSET * NLEN
    part = all_rows // n_sec
    blocks, _ = chunk_order(chips, width)

    def half(core):
        def at(i, ids, where):
            turned = (steps // blocks - 1 - i // blocks) * blocks + lax.rem(i, blocks)
            return jnp.where(where[1] == core, i, turned), 0

        return pl.BlockSpec((width, ENC_D), at)

    fixed2 = lambda i, *_: (0, 0)
    fixed3 = lambda i, *_: (0, 0, 0)
    return pl.pallas_call(
        functools.partial(layer_kernel, n_sec, chips),
        grid_spec=pltpu.PrefetchScalarGridSpec(
            num_scalar_prefetch=2,
            grid=(steps,),
            in_specs=[
                *[pl.BlockSpec((part, ENC_D), fixed2)] * n_sec,
                pl.BlockSpec((ENC_D, ENC_D), fixed2),
                pl.BlockSpec((ENC_D,), lambda i, *_: (0,)),
                pl.BlockSpec((2, width, ENC_D), lambda i, *_: (0, i, 0)),
                pl.BlockSpec((TOK_DEV, width), lambda i, *_: (0, i)),
                pl.BlockSpec((STEP, BLOCK, NBR * NLEN), lambda i, *_: (i, 0, 0)),
                pl.BlockSpec((TOK_DEV, width), lambda i, *_: (0, i)),
            ],
            out_specs=[
                pl.BlockSpec((TOK_DEV, width), lambda i, *_: (0, i)),
                half(0),
                half(1),
            ]
            + [pl.BlockSpec((part, ENC_D), fixed2)] * n_sec,
            scratch_shapes=[
                pltpu.VMEM((all_rows, ENC_D), BF16),
                pltpu.VMEM((all_rows, 2 * width), BF16),
                pltpu.VMEM((all_rows, 2 * width), F32),
                pltpu.VMEM((all_rows, 2 * width), BF16),
                pltpu.VMEM((all_rows, ENC_D), F32),
            ],
        ),
        out_shape=[
            jax.ShapeDtypeStruct((TOK_DEV, head_width), BF16),
            jax.ShapeDtypeStruct((head_width, ENC_D), BF16),
            jax.ShapeDtypeStruct((head_width, ENC_D), BF16),
        ]
        + [jax.ShapeDtypeStruct((part, ENC_D), BF16)] * n_sec,
        compiler_params=pltpu.CompilerParams(
            vmem_limit_bytes=LIMIT, dimension_semantics=("arbitrary",)
        ),
        cost_estimate=SHORT,
    )(ids, where, *rows, enc_weight, gain, weights.reshape(2, head_width, ENC_D), queries, bias, upstream)


def call(kernel, outs, *args, after=(), carry=(), scalars=0, scratch_shapes=(), cost=LONGER):
    n_in, n_out, n_extra, n_carry = len(args), len(outs), len(after), len(carry)

    def inner(*refs):
        own = refs[n_in + n_extra + n_carry:]
        kernel(*refs[:n_in], *own[:n_out], *own[n_out + n_carry:])

    vmem, anywhere = pl.BlockSpec(memory_space=pltpu.VMEM), pl.BlockSpec(memory_space=pl.ANY)
    return pl.pallas_call(
        inner,
        in_specs=[pl.BlockSpec(memory_space=pltpu.SMEM)] * scalars
        + [vmem] * (n_in - scalars)
        + [anywhere] * (n_extra + n_carry),
        out_specs=[vmem] * n_out + [anywhere] * n_carry,
        out_shape=[jax.ShapeDtypeStruct(shape, dtype) for shape, dtype in outs]
        + [jax.ShapeDtypeStruct(x.shape, x.dtype) for x in carry],
        input_output_aliases={n_in + n_extra + k: n_out + k for k in range(n_carry)},
        scratch_shapes=scratch_shapes,
        compiler_params=pltpu.CompilerParams(vmem_limit_bytes=LIMIT),
        cost_estimate=cost,
    )(*args, *after, *carry)


def split_rows(row):
    high = row.astype(BF16).astype(F32)
    at = lax.broadcasted_iota(jnp.int32, (EXTRA, row.shape[-1]), 0)
    return jnp.where(at == 0, high, jnp.where(at == 1, row - high, 0.0)).astype(BF16)


def joined(ref):
    extra = ref[pl.ds(0, EXTRA), :].astype(F32)
    return extra[0:1] + extra[1:2]


def local_kernel(rows_ref, encw_ref, gain_ref, normed_ref, inverse_ref, encoded_ref):
    normed, inverse = normalised(rows_ref[...], encw_ref)
    normed_ref[...] = normed
    inverse_ref[...] = jnp.broadcast_to(inverse, inverse_ref.shape)
    encoded_ref[...] = (normed * gain_ref[...][None, :]).astype(BF16)


def finish_kernel(*refs):
    *grads, normed_ref, inverse_ref, gain_ref, mixed_ref, send_ref = refs
    grad = grads[0][...].astype(F32)
    for g in grads[1:]:
        grad = grad + g[...].astype(F32)
    normed = normed_ref[...]
    grad_normed = grad * gain_ref[...][None, :]
    grad_mixed = inverse_ref[...][:, :1] * (
        grad_normed - normed * jnp.mean(grad_normed * normed, axis=-1, keepdims=True)
    )
    mixed_ref[...] = grad_mixed
    send_ref[pl.ds(0, EXTRA), :] = split_rows(jnp.sum(grad * normed, axis=0, keepdims=True))
    send_ref[pl.ds(EXTRA, normed.shape[0]), :] = grad_mixed.astype(BF16)


def embed_kernel(mixed_ref, encw_ref, embed_ref):
    grad_mixed = mixed_ref[...]
    embed_ref[...] = (grad_mixed + mm_nt(grad_mixed.astype(BF16), encw_ref[...])).astype(BF16)


def outer_kernel(n_sec, where, *refs):
    rows_refs, gots, (keep_ref, give_ref, total) = refs[:n_sec], refs[n_sec:2 * n_sec], refs[2 * n_sec:]
    me, odd = where[0], where[1]
    part = rows_refs[0].shape[0]
    half = keep_ref.shape[0] - EXTRA
    own = 2 * half
    raw = jnp.concatenate([r[...] for r in rows_refs], axis=0)
    low = jnp.concatenate([g[pl.ds(EXTRA, part), :] for g in gots], axis=0)
    total[...] = mm_tn(raw, low)

    def rows_of(core):
        return total[pl.ds(pl.multiple_of(me * own + core * half, 8), half), :].astype(BF16)

    keep_ref[pl.ds(EXTRA, half), :] = rows_of(odd)
    give_ref[pl.ds(EXTRA, half), :] = rows_of(1 - odd)
    rows = [joined(g) for g in gots]
    gain_row = jnp.zeros_like(rows[0])
    for s in range(n_sec):
        for k in range(n_sec):
            here = lax.rem(me + n_sec - k, n_sec) == s
            gain_row = gain_row + jnp.where(here, rows[k], 0.0)
    extra = split_rows(gain_row)
    keep_ref[pl.ds(0, EXTRA), :] = extra
    give_ref[pl.ds(0, EXTRA), :] = extra


def merge_kernel(*refs):
    *ins, out_ref = refs
    half = out_ref.shape[0] - EXTRA
    gains = [joined(r) for r in ins]
    weights = [r[pl.ds(EXTRA, half), :].astype(F32) for r in ins]
    while len(gains) > 1:
        gains = [a + b for a, b in zip(gains[::2], gains[1::2])]
        weights = [a + b for a, b in zip(weights[::2], weights[1::2])]
    out_ref[pl.ds(0, EXTRA), :] = split_rows(gains[0])
    out_ref[pl.ds(EXTRA, half), :] = weights[0].astype(BF16)


def merged(*parts, **order):
    return call(merge_kernel, [(parts[0].shape, BF16)], *parts, **order)


def spread_kernel(where, own_ref, inc_ref, weight_ref, gain_ref):
    half = own_ref.shape[0] - EXTRA
    odd = where[1]
    for ref, at in ((own_ref, odd), (inc_ref, 1 - odd)):
        weight_ref[pl.ds(pl.multiple_of(at * half, 8), half), :] = ref[pl.ds(EXTRA, half), :].astype(F32)
    gain_ref[...] = joined(own_ref)[0]


def sum_kernel(plan, cut, where, *refs):
    n = len(plan)
    count = sum(arrays for arrays, _, _ in plan)
    sources, (out_ref, held, total, in_sems, out_sems) = refs[:count], refs[-5:]
    rows = out_ref.shape[0]
    size = rows // cut

    def fetch(k, c, which=0):
        start = sum(arrays for arrays, _, _ in plan[:k])
        block = plan[k][1]
        base = 0 if block is None else pl.multiple_of(where[block] * rows, rows)
        source = sources[start + which].at[pl.ds(base + c * size, size), :]
        return pltpu.make_async_copy(source, held.at[k, pl.ds(c * size, size), :], in_sems.at[k, c])

    def store(c):
        span = pl.ds(c * size, size)
        return pltpu.make_async_copy(total.at[span, :], out_ref.at[span, :], out_sems.at[c])

    for c in range(cut):
        for k, (arrays, _, choice) in enumerate(plan):
            if arrays == 1:
                fetch(k, c).start()
                continue
            for which in range(arrays):
                pl.when(where[choice] == which)(fetch(k, c, which).start)
    for c in range(cut):
        for k in range(n):
            fetch(k, c).wait()
        span = pl.ds(c * size, size)
        value = held[0, span, :].astype(F32)
        for k in range(1, n):
            value = value + held[k, span, :].astype(F32)
        total[span, :] = value.astype(total.dtype)
        store(c).start()
    for c in range(cut):
        store(c).wait()


def block_sum(rows, dtype, where, *terms, after=()):
    cut = (4 if dtype == F32 else 2) if rows % 64 == 0 else 1
    n = len(terms)
    sources = [x for arrays, _, _ in terms for x in arrays] + list(after)
    anywhere = pl.BlockSpec(memory_space=pl.ANY)
    return pl.pallas_call(
        functools.partial(sum_kernel, [(len(arrays), block, choice) for arrays, block, choice in terms], cut),
        in_specs=[pl.BlockSpec(memory_space=pltpu.SMEM)] + [anywhere] * len(sources),
        out_specs=anywhere,
        out_shape=jax.ShapeDtypeStruct((rows, ENC_D), dtype),
        scratch_shapes=[
            pltpu.VMEM((n, rows, ENC_D), BF16),
            pltpu.VMEM((rows, ENC_D), dtype),
            pltpu.SemaphoreType.DMA((n, cut)),
            pltpu.SemaphoreType.DMA((cut,)),
        ],
        compiler_params=pltpu.CompilerParams(vmem_limit_bytes=LIMIT),
        cost_estimate=SHORT,
    )(where, *sources)


def rotated(x, n, k):
    return lax.ppermute(x, "section", [(i, (i + k) % n) for i in range(n)]) if k else x


def chunk_at(chips, chip, step, core):
    place = jnp.where(core == 0, chip, chips - 1 - chip)
    ahead = jnp.minimum(chips - step + place, chips - 1)
    return jnp.where(core == 0, ahead, chips - 1 - ahead)


def body(n_sec, n_dp, nbr_embed, enc_weight, enc_gain, kv_weight, queries, pos_bias, nbr_ids, ctx_grad):
    local_rows = nbr_embed[0].reshape(-1, ENC_D)
    part = local_rows.shape[0]
    own = ENC_D // n_sec
    half = own // 2
    chips = n_dp // 2
    kv_rows = 2 * HEADS * HEAD // n_dp
    me = lax.axis_index("section")
    rank = lax.axis_index("dp")
    chip, core = rank // 2, lax.rem(rank, 2)
    near = [(i, i ^ 1) for i in range(n_dp)]

    early = chips // 2
    where, places = [me, core], {}

    def place(name, chunk, lane):
        keyed = chunk < chips // 2
        spot = jnp.where(keyed, chunk, chips - 1 - chunk)
        mine = jnp.where(keyed, core, 1 - core)
        places[name] = range(len(where), len(where) + 3)
        where.extend([2 * spot + lane, mine, 1 - mine])

    for step in range(1, chips):
        for j, lane in enumerate((1 - core, core)):
            place((step, j), chunk_at(chips, chip, step, core), lane)
    place("other", chip, 1 - core)
    place("own", chip, core)
    where = jnp.stack(where).astype(jnp.int32)
    spot = jnp.stack([me, core]).astype(jnp.int32)

    rows = [rotated(local_rows, n_sec, k) for k in range(n_sec)]
    normed, inverse, encoded = call(
        local_kernel,
        [((part, ENC_D), F32), ((part, HEAD), F32), ((part, ENC_D), BF16)],
        local_rows, enc_weight, enc_gain, after=[spot],
    )
    grad_query, first, second, *grad_enc = layer(
        n_sec, chips, nbr_ids[0], where, [encoded] + rows[1:], enc_weight, enc_gain, kv_weight[0], queries[0], pos_bias[0], ctx_grad[0]
    )
    got = [rotated(grad_enc[k], n_sec, k) for k in range(n_sec)]
    incoming = [None, None]
    state = {"where": where, "sums": []}
    mine = [first, second]
    theirs = [lax.ppermute(x, "dp", near) for x in mine]

    def kv_step(step, lanes=(0, 1)):
        hops = [(2 * a, 2 * a + 2) for a in range(step)]
        hops += [(2 * (chips - 1 - a) + 1, 2 * (chips - 2 - a) + 1) for a in range(step)]
        for j in lanes:
            block, here, there = places[step, j]
            if step <= early:
                terms = [(mine[1:], block, None), (theirs[:1], block, None)]
            else:
                terms = [(mine, block, here), (theirs, block, there)]
            if incoming[j] is not None:
                terms.append(([incoming[j]], None, None))
            out = block_sum(kv_rows, BF16, state["where"], *terms, after=state["sums"][-j:] if j else ())
            incoming[j] = lax.ppermute(out, "dp", hops)
            state["sums"].append(out)

    def last_pair():
        block, here, _ = places["other"]
        terms = [(mine, block, here), ([incoming[0]], None, None)]
        out = block_sum(kv_rows, BF16, state["where"], *terms)
        state["swapped"] = lax.ppermute(out, "dp", near)
        state["sums"].append(out)

    def order():
        sums, state["sums"] = state["sums"], []
        return {"after": sums, "carry": [state["where"]]}

    def finish_stage():
        held = order()
        held["after"] = held["after"] + theirs[1:]
        state["mixed"], send, state["where"] = call(
            finish_kernel,
            [((part, ENC_D), F32), ((EXTRA + part, ENC_D), BF16)],
            *got, normed, inverse, enc_gain, **held,
        )
        state["lows"] = [rotated(send, n_sec, k) for k in range(n_sec)]

    def outer_stage():
        shape = ((EXTRA + half, ENC_D), BF16)
        *state["halves"], state["where"] = call(
            functools.partial(outer_kernel, n_sec),
            [shape, shape],
            spot, *rows, *state["lows"],
            scalars=1,
            scratch_shapes=[pltpu.VMEM((ENC_D, ENC_D), F32)],
            **order(),
        )

    def swap(x, dist):
        return lax.ppermute(x, "dp", [(i, i ^ dist) for i in range(n_dp)])

    def pair_stage():
        keep, give = state["halves"]
        state["payload"], state["where"] = merged(keep, swap(give, 1), cost=SHORT, **order())

    def embed_stage():
        (state["embed"],) = call(embed_kernel, [((part, ENC_D), BF16)], state["mixed"], enc_weight, after=[state["payload"]], cost=LONGER)

    def merge_stage(dist):
        payload = state["payload"]
        state["payload"], state["where"] = merged(payload, swap(payload, dist), cost=LONGER if dist == 2 else LONGER, **order())

    merges = [functools.partial(merge_stage, 2 << k) for k in range((chips - 1).bit_length())]
    enc_chain = [finish_stage, outer_stage, pair_stage] + merges
    kv_chain = [functools.partial(kv_step, step) for step in range(1, min(chips, 3))]
    kv_chain += [functools.partial(kv_step, step, (j,)) for step in range(3, chips) for j in range(2)] + [last_pair]
    for at in range(max(len(kv_chain), len(enc_chain))):
        for chain in (kv_chain, enc_chain):
            if at < len(chain):
                chain[at]()
        if at == 3:
            embed_stage()
    payload = state["payload"]
    other = lax.ppermute(payload, "dp", near)
    held = order()
    weight_grad, gain_row, table = call(
        spread_kernel, [((own, ENC_D), F32), ((ENC_D,), F32)], spot, payload, other, scalars=1, cost=SHORT, **held,
    )
    block, here, _ = places["own"]
    kv_grad = block_sum(
        kv_rows, F32, table, (mine, block, here), ([state["swapped"]], None, None), ([incoming[1]], None, None)
    )
    embed_grad = state["embed"]
    return (
        grad_query[None],
        kv_grad[None],
        weight_grad,
        gain_row,
        embed_grad.reshape(nbr_embed.shape),
    )


def solution(mesh):
    return jax.shard_map(
        functools.partial(body, mesh.shape["section"], mesh.shape["dp"]),
        mesh=mesh,
        in_specs=(
            P("dp", None, "section", None),
            P(),
            P(),
            P("section", None, None),
            P("section", "dp", None),
            P("section", None, None, None),
            P("dp", None, None),
            P("section", "dp", None),
        ),
        out_specs=(
            P("section", "dp", None),
            P("section", "dp", None),
            P("section", None),
            P(),
            P("dp", None, "section", None),
        ),
        check_vma=False,
    )
```

```python
import functools
import math

import jax
import jax.numpy as jnp
from jax import lax
from jax.experimental import pallas as pl
from jax.experimental.pallas import tpu as pltpu
from jax.sharding import PartitionSpec as P

HEADS = 16
HEAD = 128
ENC_D = 896
BLOCK = 64
NBR = 2
NLEN = 128
TOK_DEV = 128
NSET = 4
PAIR = 2
STEP = 4
EXTRA = 16

eps_norm = 1e-06
LIMIT = 65400 * 1024
SHORT = pl.CostEstimate(flops=1, bytes_accessed=1, transcendentals=0)
LONGER = pl.CostEstimate(flops=20_000_000_000, bytes_accessed=1_000_000, transcendentals=0)
F32 = jnp.float32
BF16 = jnp.bfloat16


def mm(a, b):
    return lax.dot_general(a, b, (((1,), (0,)), ((), ())), preferred_element_type=F32)


def mm_nt(a, b):
    return lax.dot_general(a, b, (((1,), (1,)), ((), ())), preferred_element_type=F32)


def mm_tn(a, b):
    return lax.dot_general(a, b, (((0,), (0,)), ((), ())), preferred_element_type=F32)


def chunk_order(chips, width):
    rows = 2 * HEADS * HEAD // chips
    return max(1, rows // width), max(1, width // rows)


def normalised(raw, encw_ref):
    mixed = raw.astype(F32) + mm(raw, encw_ref[...])
    inverse = lax.rsqrt(jnp.mean(mixed * mixed, axis=-1, keepdims=True) + eps_norm)
    return mixed * inverse, inverse


def layer_kernel(
    n_sec, chips, ids, where, *refs,
):
    rows_refs, (encw_ref, gain_ref, w_ref, q_ref, bias_ref, up_ref) = refs[:n_sec], refs[n_sec:n_sec + 6]
    qg_ref, first_ref, second_ref, *rest = refs[n_sec + 6:]
    ge_refs, (enc, proj, total, gset, acc) = rest[:n_sec], rest[n_sec:]
    step = pl.program_id(0)
    part = NLEN // n_sec
    blocks = TOK_DEV // BLOCK
    width = STEP * HEAD
    factor = 1.0 / math.sqrt(HEAD)

    @pl.when(step == 0)
    def _():
        def places(k):
            s = lax.rem(where[0] + n_sec - k, n_sec)
            return [(e, pl.ds(pl.multiple_of(e * NLEN + s * part, part), part)) for e in range(NSET)]

        others = jnp.concatenate([r[...] for r in rows_refs[1:]], axis=0)
        normed, _ = normalised(others, encw_ref)
        encoded = (normed * gain_ref[...][None, :]).astype(BF16)
        for e, span in places(0):
            enc[span, :] = rows_refs[0][pl.ds(e * part, part), :]
        for k in range(1, n_sec):
            for e, span in places(k):
                at = ((k - 1) * NSET + e) * part
                enc[span, :] = encoded[at:at + part]

    encoded = enc[...]
    weights = w_ref[...].reshape(2 * width, ENC_D)
    proj[...] = mm_nt(encoded, weights).astype(BF16)
    spans = [
        [pl.ds(pl.multiple_of(ids[c, n] * NLEN, NLEN), NLEN) for n in range(NBR)]
        for c in range(blocks)
    ]
    toks = [slice(c * BLOCK, (c + 1) * BLOCK) for c in range(blocks)]
    pair = PAIR * HEAD
    items = [(c, g) for c in range(blocks) for g in range(STEP // PAIR)]

    def stacked(ref, c, g):
        x = ref[toks[c], g * pair:(g + 1) * pair]
        head_of = lax.broadcasted_iota(jnp.int32, x.shape, 1) // HEAD
        return jnp.concatenate([jnp.where(head_of == h, x, jnp.zeros_like(x)) for h in range(PAIR)], axis=0)

    def picked(c, g, base):
        return jnp.concatenate([proj[s, base + g * pair:base + (g + 1) * pair] for s in spans[c]], axis=0)

    def bias(g):
        return jnp.concatenate([bias_ref[g * PAIR + h] for h in range(PAIR)], axis=0).astype(F32)

    keys = {i: picked(*i, 0) for i in items}
    values = {i: picked(*i, width) for i in items}
    query = {i: stacked(q_ref, *i) for i in items}
    upstream = {i: stacked(up_ref, *i) for i in items}
    scores = {i: mm_nt(query[i], keys[i]) * factor + bias(i[1]) for i in items}
    dprobs = {i: mm_nt(upstream[i], values[i]) for i in items}
    exps = {i: jnp.exp(scores[i] - jnp.max(scores[i], axis=-1, keepdims=True)) for i in items}
    probs = {i: exps[i] / jnp.sum(exps[i], axis=-1, keepdims=True) for i in items}
    dvalues = {i: mm_tn(probs[i].astype(BF16), upstream[i]) for i in items}
    inner = {i: jnp.sum(probs[i] * dprobs[i], axis=-1, keepdims=True) for i in items}
    dscores = {i: (probs[i] * (dprobs[i] - inner[i])).astype(BF16) for i in items}
    dkeys = {i: mm_tn(dscores[i], query[i]) * factor for i in items}
    dquery = {i: mm(dscores[i], keys[i]) * factor for i in items}
    for c, g in items:
        for h in range(PAIR):
            col = slice(h * HEAD, (h + 1) * HEAD)
            qg_ref[toks[c], g * pair + h * HEAD:g * pair + (h + 1) * HEAD] = (
                dquery[c, g][h * BLOCK:(h + 1) * BLOCK, col].astype(BF16)
            )
        for base, grads in ((0, dkeys[c, g]), (width, dvalues[c, g])):
            cols = slice(base + g * pair, base + (g + 1) * pair)
            parts = [grads[n * NLEN:(n + 1) * NLEN] for n in range(NBR)]
            if c > 0:
                for n, s in enumerate(spans[c]):
                    total[s, cols] += parts[n]
                continue
            for e in range(NSET):
                picked_parts = [jnp.where(ids[c, n] == e, parts[n], 0.0) for n in range(NBR)]
                total[e * NLEN:(e + 1) * NLEN, cols] = sum(picked_parts[1:], picked_parts[0])
    gset[...] = total[...].astype(BF16)
    acc[...] = jnp.where(step == 0, 0.0, acc[...]) + mm(gset[...], weights)
    kv = mm_tn(gset[...], encoded).astype(BF16)
    keys_part, values_part = kv[:width], kv[width:]
    _, inside = chunk_order(chips, width)
    size = width // inside
    values_part = jnp.concatenate([values_part[u * size:(u + 1) * size] for u in reversed(range(inside))], axis=0)
    low = where[1] == 0
    first_ref[...] = jnp.where(low, keys_part, values_part)
    second_ref[...] = jnp.where(low, values_part, keys_part)

    @pl.when(step == pl.num_programs(0) - 1)
    def _():
        for k in range(n_sec):
            s = lax.rem(where[0] + k, n_sec)
            for e in range(NSET):
                span = pl.ds(pl.multiple_of(e * NLEN + s * part, part), part)
                ge_refs[k][pl.ds(e * part, part), :] = acc[span, :].astype(BF16)


def layer(n_sec, chips, ids, where, rows, enc_weight, gain, weights, queries, bias, upstream):
    head_width = HEADS * HEAD
    width = STEP * HEAD
    steps = HEADS // STEP
    all_rows = NSET * NLEN
    part = all_rows // n_sec
    blocks, _ = chunk_order(chips, width)

    def half(core):
        def at(i, ids, where):
            turned = (steps // blocks - 1 - i // blocks) * blocks + lax.rem(i, blocks)
            return jnp.where(where[1] == core, i, turned), 0

        return pl.BlockSpec((width, ENC_D), at)

    fixed2 = lambda i, *_: (0, 0)
    fixed3 = lambda i, *_: (0, 0, 0)
    return pl.pallas_call(
        functools.partial(layer_kernel, n_sec, chips),
        grid_spec=pltpu.PrefetchScalarGridSpec(
            num_scalar_prefetch=2,
            grid=(steps,),
            in_specs=[
                *[pl.BlockSpec((part, ENC_D), fixed2)] * n_sec,
                pl.BlockSpec((ENC_D, ENC_D), fixed2),
                pl.BlockSpec((ENC_D,), lambda i, *_: (0,)),
                pl.BlockSpec((2, width, ENC_D), lambda i, *_: (0, i, 0)),
                pl.BlockSpec((TOK_DEV, width), lambda i, *_: (0, i)),
                pl.BlockSpec((STEP, BLOCK, NBR * NLEN), lambda i, *_: (i, 0, 0)),
                pl.BlockSpec((TOK_DEV, width), lambda i, *_: (0, i)),
            ],
            out_specs=[
                pl.BlockSpec((TOK_DEV, width), lambda i, *_: (0, i)),
                half(0),
                half(1),
            ]
            + [pl.BlockSpec((part, ENC_D), fixed2)] * n_sec,
            scratch_shapes=[
                pltpu.VMEM((all_rows, ENC_D), BF16),
                pltpu.VMEM((all_rows, 2 * width), BF16),
                pltpu.VMEM((all_rows, 2 * width), F32),
                pltpu.VMEM((all_rows, 2 * width), BF16),
                pltpu.VMEM((all_rows, ENC_D), F32),
            ],
        ),
        out_shape=[
            jax.ShapeDtypeStruct((TOK_DEV, head_width), BF16),
            jax.ShapeDtypeStruct((head_width, ENC_D), BF16),
            jax.ShapeDtypeStruct((head_width, ENC_D), BF16),
        ]
        + [jax.ShapeDtypeStruct((part, ENC_D), BF16)] * n_sec,
        compiler_params=pltpu.CompilerParams(
            vmem_limit_bytes=LIMIT, dimension_semantics=("arbitrary",)
        ),
        cost_estimate=SHORT,
    )(ids, where, *rows, enc_weight, gain, weights.reshape(2, head_width, ENC_D), queries, bias, upstream)


def call(kernel, outs, *args, after=(), carry=(), scalars=0, scratch_shapes=(), cost=LONGER):
    n_in, n_out, n_extra, n_carry = len(args), len(outs), len(after), len(carry)

    def inner(*refs):
        own = refs[n_in + n_extra + n_carry:]
        kernel(*refs[:n_in], *own[:n_out], *own[n_out + n_carry:])

    vmem, anywhere = pl.BlockSpec(memory_space=pltpu.VMEM), pl.BlockSpec(memory_space=pl.ANY)
    return pl.pallas_call(
        inner,
        in_specs=[pl.BlockSpec(memory_space=pltpu.SMEM)] * scalars
        + [vmem] * (n_in - scalars)
        + [anywhere] * (n_extra + n_carry),
        out_specs=[vmem] * n_out + [anywhere] * n_carry,
        out_shape=[jax.ShapeDtypeStruct(shape, dtype) for shape, dtype in outs]
        + [jax.ShapeDtypeStruct(x.shape, x.dtype) for x in carry],
        input_output_aliases={n_in + n_extra + k: n_out + k for k in range(n_carry)},
        scratch_shapes=scratch_shapes,
        compiler_params=pltpu.CompilerParams(vmem_limit_bytes=LIMIT),
        cost_estimate=cost,
    )(*args, *after, *carry)


def split_rows(row):
    high = row.astype(BF16).astype(F32)
    at = lax.broadcasted_iota(jnp.int32, (EXTRA, row.shape[-1]), 0)
    return jnp.where(at == 0, high, jnp.where(at == 1, row - high, 0.0)).astype(BF16)


def joined(ref):
    extra = ref[pl.ds(0, EXTRA), :].astype(F32)
    return extra[0:1] + extra[1:2]


def local_kernel(rows_ref, encw_ref, gain_ref, normed_ref, inverse_ref, encoded_ref):
    normed, inverse = normalised(rows_ref[...], encw_ref)
    normed_ref[...] = normed
    inverse_ref[...] = jnp.broadcast_to(inverse, inverse_ref.shape)
    encoded_ref[...] = (normed * gain_ref[...][None, :]).astype(BF16)


def finish_kernel(*refs):
    *grads, normed_ref, inverse_ref, gain_ref, mixed_ref, send_ref = refs
    grad = grads[0][...].astype(F32)
    for g in grads[1:]:
        grad = grad + g[...].astype(F32)
    normed = normed_ref[...]
    grad_normed = grad * gain_ref[...][None, :]
    grad_mixed = inverse_ref[...][:, :1] * (
        grad_normed - normed * jnp.mean(grad_normed * normed, axis=-1, keepdims=True)
    )
    mixed_ref[...] = grad_mixed
    send_ref[pl.ds(0, EXTRA), :] = split_rows(jnp.sum(grad * normed, axis=0, keepdims=True))
    send_ref[pl.ds(EXTRA, normed.shape[0]), :] = grad_mixed.astype(BF16)


def embed_kernel(mixed_ref, encw_ref, embed_ref):
    grad_mixed = mixed_ref[...]
    embed_ref[...] = (grad_mixed + mm_nt(grad_mixed.astype(BF16), encw_ref[...])).astype(BF16)


def outer_kernel(n_sec, where, *refs):
    rows_refs, gots, (keep_ref, give_ref, total) = refs[:n_sec], refs[n_sec:2 * n_sec], refs[2 * n_sec:]
    me, odd = where[0], where[1]
    part = rows_refs[0].shape[0]
    half = keep_ref.shape[0] - EXTRA
    own = 2 * half
    raw = jnp.concatenate([r[...] for r in rows_refs], axis=0)
    low = jnp.concatenate([g[pl.ds(EXTRA, part), :] for g in gots], axis=0)
    total[...] = mm_tn(raw, low)

    def rows_of(core):
        return total[pl.ds(pl.multiple_of(me * own + core * half, 8), half), :].astype(BF16)

    keep_ref[pl.ds(EXTRA, half), :] = rows_of(odd)
    give_ref[pl.ds(EXTRA, half), :] = rows_of(1 - odd)
    rows = [joined(g) for g in gots]
    gain_row = jnp.zeros_like(rows[0])
    for s in range(n_sec):
        for k in range(n_sec):
            here = lax.rem(me + n_sec - k, n_sec) == s
            gain_row = gain_row + jnp.where(here, rows[k], 0.0)
    extra = split_rows(gain_row)
    keep_ref[pl.ds(0, EXTRA), :] = extra
    give_ref[pl.ds(0, EXTRA), :] = extra


def merge_kernel(*refs):
    *ins, out_ref = refs
    half = out_ref.shape[0] - EXTRA
    gains = [joined(r) for r in ins]
    weights = [r[pl.ds(EXTRA, half), :].astype(F32) for r in ins]
    while len(gains) > 1:
        gains = [a + b for a, b in zip(gains[::2], gains[1::2])]
        weights = [a + b for a, b in zip(weights[::2], weights[1::2])]
    out_ref[pl.ds(0, EXTRA), :] = split_rows(gains[0])
    out_ref[pl.ds(EXTRA, half), :] = weights[0].astype(BF16)


def merged(*parts, **order):
    return call(merge_kernel, [(parts[0].shape, BF16)], *parts, **order)


def spread_kernel(where, own_ref, inc_ref, weight_ref, gain_ref):
    half = own_ref.shape[0] - EXTRA
    odd = where[1]
    for ref, at in ((own_ref, odd), (inc_ref, 1 - odd)):
        weight_ref[pl.ds(pl.multiple_of(at * half, 8), half), :] = ref[pl.ds(EXTRA, half), :].astype(F32)
    gain_ref[...] = joined(own_ref)[0]


def sum_kernel(plan, cut, where, *refs):
    n = len(plan)
    count = sum(arrays for arrays, _, _ in plan)
    sources, (out_ref, held, total, in_sems, out_sems) = refs[:count], refs[-5:]
    rows = out_ref.shape[0]
    size = rows // cut

    def fetch(k, c, which=0):
        start = sum(arrays for arrays, _, _ in plan[:k])
        block = plan[k][1]
        base = 0 if block is None else pl.multiple_of(where[block] * rows, rows)
        source = sources[start + which].at[pl.ds(base + c * size, size), :]
        return pltpu.make_async_copy(source, held.at[k, pl.ds(c * size, size), :], in_sems.at[k, c])

    def store(c):
        span = pl.ds(c * size, size)
        return pltpu.make_async_copy(total.at[span, :], out_ref.at[span, :], out_sems.at[c])

    for c in range(cut):
        for k, (arrays, _, choice) in enumerate(plan):
            if arrays == 1:
                fetch(k, c).start()
                continue
            for which in range(arrays):
                pl.when(where[choice] == which)(fetch(k, c, which).start)
    for c in range(cut):
        for k in range(n):
            fetch(k, c).wait()
        span = pl.ds(c * size, size)
        value = held[0, span, :].astype(F32)
        for k in range(1, n):
            value = value + held[k, span, :].astype(F32)
        total[span, :] = value.astype(total.dtype)
        store(c).start()
    for c in range(cut):
        store(c).wait()


def block_sum(rows, dtype, where, *terms, after=()):
    cut = (4 if dtype == F32 else 2) if rows % 64 == 0 else 1
    n = len(terms)
    sources = [x for arrays, _, _ in terms for x in arrays] + list(after)
    anywhere = pl.BlockSpec(memory_space=pl.ANY)
    return pl.pallas_call(
        functools.partial(sum_kernel, [(len(arrays), block, choice) for arrays, block, choice in terms], cut),
        in_specs=[pl.BlockSpec(memory_space=pltpu.SMEM)] + [anywhere] * len(sources),
        out_specs=anywhere,
        out_shape=jax.ShapeDtypeStruct((rows, ENC_D), dtype),
        scratch_shapes=[
            pltpu.VMEM((n, rows, ENC_D), BF16),
            pltpu.VMEM((rows, ENC_D), dtype),
            pltpu.SemaphoreType.DMA((n, cut)),
            pltpu.SemaphoreType.DMA((cut,)),
        ],
        compiler_params=pltpu.CompilerParams(vmem_limit_bytes=LIMIT),
        cost_estimate=SHORT,
    )(where, *sources)


def rotated(x, n, k):
    return lax.ppermute(x, "section", [(i, (i + k) % n) for i in range(n)]) if k else x


def chunk_at(chips, chip, step, core):
    place = jnp.where(core == 0, chip, chips - 1 - chip)
    ahead = jnp.minimum(chips - step + place, chips - 1)
    return jnp.where(core == 0, ahead, chips - 1 - ahead)


def body(n_sec, n_dp, nbr_embed, enc_weight, enc_gain, kv_weight, queries, pos_bias, nbr_ids, ctx_grad):
    local_rows = nbr_embed[0].reshape(-1, ENC_D)
    part = local_rows.shape[0]
    own = ENC_D // n_sec
    half = own // 2
    chips = n_dp // 2
    kv_rows = 2 * HEADS * HEAD // n_dp
    me = lax.axis_index("section")
    rank = lax.axis_index("dp")
    chip, core = rank // 2, lax.rem(rank, 2)
    near = [(i, i ^ 1) for i in range(n_dp)]

    early = chips // 2
    where, places = [me, core], {}

    def place(name, chunk, lane):
        keyed = chunk < chips // 2
        spot = jnp.where(keyed, chunk, chips - 1 - chunk)
        mine = jnp.where(keyed, core, 1 - core)
        places[name] = range(len(where), len(where) + 3)
        where.extend([2 * spot + lane, mine, 1 - mine])

    for step in range(1, chips):
        for j, lane in enumerate((1 - core, core)):
            place((step, j), chunk_at(chips, chip, step, core), lane)
    place("other", chip, 1 - core)
    place("own", chip, core)
    where = jnp.stack(where).astype(jnp.int32)
    spot = jnp.stack([me, core]).astype(jnp.int32)

    rows = [rotated(local_rows, n_sec, k) for k in range(n_sec)]
    normed, inverse, encoded = call(
        local_kernel,
        [((part, ENC_D), F32), ((part, HEAD), F32), ((part, ENC_D), BF16)],
        local_rows, enc_weight, enc_gain, after=[spot],
    )
    grad_query, first, second, *grad_enc = layer(
        n_sec, chips, nbr_ids[0], where, [encoded] + rows[1:], enc_weight, enc_gain, kv_weight[0], queries[0], pos_bias[0], ctx_grad[0]
    )
    got = [rotated(grad_enc[k], n_sec, k) for k in range(n_sec)]
    incoming = [None, None]
    state = {"where": where, "sums": []}
    mine = [first, second]
    theirs = [lax.ppermute(x, "dp", near) for x in mine]

    def kv_step(step, lanes=(0, 1)):
        hops = [(2 * a, 2 * a + 2) for a in range(step)]
        hops += [(2 * (chips - 1 - a) + 1, 2 * (chips - 2 - a) + 1) for a in range(step)]
        for j in lanes:
            block, here, there = places[step, j]
            if step <= early:
                terms = [(mine[1:], block, None), (theirs[:1], block, None)]
            else:
                terms = [(mine, block, here), (theirs, block, there)]
            if incoming[j] is not None:
                terms.append(([incoming[j]], None, None))
            out = block_sum(kv_rows, BF16, state["where"], *terms, after=state["sums"][-j:] if j else ())
            incoming[j] = lax.ppermute(out, "dp", hops)
            state["sums"].append(out)

    def last_pair():
        block, here, _ = places["other"]
        terms = [(mine, block, here), ([incoming[0]], None, None)]
        out = block_sum(kv_rows, BF16, state["where"], *terms)
        state["swapped"] = lax.ppermute(out, "dp", near)
        state["sums"].append(out)

    def order():
        sums, state["sums"] = state["sums"], []
        return {"after": sums, "carry": [state["where"]]}

    def finish_stage():
        held = order()
        held["after"] = held["after"] + theirs[1:]
        state["mixed"], send, state["where"] = call(
            finish_kernel,
            [((part, ENC_D), F32), ((EXTRA + part, ENC_D), BF16)],
            *got, normed, inverse, enc_gain, **held,
        )
        state["lows"] = [rotated(send, n_sec, k) for k in range(n_sec)]

    def outer_stage():
        shape = ((EXTRA + half, ENC_D), BF16)
        *state["halves"], state["where"] = call(
            functools.partial(outer_kernel, n_sec),
            [shape, shape],
            spot, *rows, *state["lows"],
            scalars=1,
            scratch_shapes=[pltpu.VMEM((ENC_D, ENC_D), F32)],
            **order(),
        )

    def swap(x, dist):
        return lax.ppermute(x, "dp", [(i, i ^ dist) for i in range(n_dp)])

    def pair_stage():
        keep, give = state["halves"]
        state["payload"], state["where"] = merged(keep, swap(give, 1), cost=SHORT, **order())

    def embed_stage():
        (state["embed"],) = call(embed_kernel, [((part, ENC_D), BF16)], state["mixed"], enc_weight, after=[state["payload"]], cost=LONGER)

    def merge_stage(dist):
        payload = state["payload"]
        state["payload"], state["where"] = merged(payload, swap(payload, dist), cost=LONGER if dist == 2 else LONGER, **order())

    merges = [functools.partial(merge_stage, 2 << k) for k in range((chips - 1).bit_length())]
    enc_chain = [finish_stage, outer_stage, pair_stage] + merges
    kv_chain = [functools.partial(kv_step, step) for step in range(1, min(chips, 3))]
    kv_chain += [functools.partial(kv_step, step, (j,)) for step in range(3, chips) for j in range(2)] + [last_pair]
    for at in range(max(len(kv_chain), len(enc_chain))):
        for chain in (kv_chain, enc_chain):
            if at < len(chain):
                chain[at]()
        if at == 3:
            embed_stage()
    payload = state["payload"]
    other = lax.ppermute(payload, "dp", near)
    held = order()
    weight_grad, gain_row, table = call(
        spread_kernel, [((own, ENC_D), F32), ((ENC_D,), F32)], spot, payload, other, scalars=1, cost=SHORT, **held,
    )
    block, here, _ = places["own"]
    kv_grad = block_sum(
        kv_rows, F32, table, (mine, block, here), ([state["swapped"]], None, None), ([incoming[1]], None, None)
    )
    embed_grad = state["embed"]
    return (
        grad_query[None],
        kv_grad[None],
        weight_grad,
        gain_row,
        embed_grad.reshape(nbr_embed.shape),
    )


def solution(mesh):
    return jax.shard_map(
        functools.partial(body, mesh.shape["section"], mesh.shape["dp"]),
        mesh=mesh,
        in_specs=(
            P("dp", None, "section", None),
            P(),
            P(),
            P("section", None, None),
            P("section", "dp", None),
            P("section", None, None, None),
            P("dp", None, None),
            P("section", "dp", None),
        ),
        out_specs=(
            P("section", "dp", None),
            P("section", "dp", None),
            P("section", None),
            P(),
            P("dp", None, "section", None),
        ),
        check_vma=False,
    )
```
